32 devices in a mesh: ens: 4 (over z), lon: 2 (over y), lat: 4 (over x, core).
Axes of the slice: x: 2, y: 2, z: 4, core: 2. Of those that a mesh axis runs over, the one named last changes fastest.
Arguments:
- ocean_state: bfloat16 [4, 200, 32, 256], P('ens', None, 'lat', 'lon'), may hold values from -6 to 6
- ocean_mask: int32 [32, 256], P('lat', 'lon'), may hold values from 0 to 1, as said below
- dw_weight: float32 [200, 49], replicated, may hold values from -0.875 to 0.875
- norm_gain: float32 [200], replicated, may hold values from 0.1 to 1.9
- expand_weight: bfloat16 [200, 800], replicated, may hold values from -0.4375 to 0.4375
- reduce_weight: bfloat16 [800, 200], replicated, may hold values from -0.21875 to 0.21875
- cotangent: bfloat16 [4, 200, 32, 256], P('ens', None, 'lat', 'lon'), may hold values from -6 to 6
Outputs:
- next_state: bfloat16 [4, 200, 32, 256], P('ens', None, 'lat', 'lon')
- grad_depthwise: float32 [200, 49], replicated
- grad_gain: float32 [200], replicated
- grad_expand: float32 [200, 800], replicated
- grad_reduce: float32 [800, 200], replicated
The draws below stay inside these ranges and needn't reach their ends.
Inputs may be any that keep to these rules, and one draw needn't show every extreme that they name: `ocean_mask`: the share of ocean cells differs from tile to tile of 8 x 128 cells, from about a third to nearly all.
All inputs are finite; a program needn't handle non-finite values.
Results may differ from the reference program's by a relative error of at most 0.0058.
Values may be sent and summed in bfloat16 or wider, within the bound.
A program may use at most 64 MiB of HBM per device.

```python
import math
import jax
import jax.numpy as jnp
from jax import lax

C = 200
HID = 800
KS = 7
TH = 8
TW = 128
ENS = 4
NY = 32
NX = 256


def draw_ocean_mask(key, part):
    tile_key = jax.random.fold_in(key, 11)
    cell_key = jax.random.fold_in(key, 12)
    ocean_share = jax.random.randint(tile_key, (NY // TH, NX // TW), 30, 101)
    ocean_share = jnp.repeat(jnp.repeat(ocean_share, TH, axis=0), TW, axis=1)
    cell_draw = jax.random.randint(cell_key, (NY, NX), 0, 100)
    return jnp.where(cell_draw < ocean_share, 1, 0).astype(jnp.int32)


def shard_levels(rng, shape, cuts, smallest, high):
    def one(axis_at, blocks):
        heights = jax.random.uniform(jax.random.fold_in(jax.random.fold_in(rng, 6), axis_at), (blocks,), jnp.float32, smallest / len(cuts), high / len(cuts))
        return jnp.repeat(jnp.exp(heights), shape[axis_at] // blocks).reshape((-1,) + (1,) * (len(shape) - axis_at - 1))

    level = one(*cuts[0])
    for cut in cuts[1:]:
        level = level * one(*cut)
    return level


def gaussian(own_key, extent, scale, most, split=(), dtype=jnp.bfloat16):
    array = jax.random.normal(own_key, extent, jnp.float32) * scale
    if len(split) > 0:
        array = shard_levels(own_key, extent, split, -0.22, 0.18) * array
    return jnp.clip(array, min=-most, max=most).astype(dtype)


def setup_inputs(seed: int = 0) -> dict:
    streams_of = jax.random.split(jax.random.key(seed), 8)
    return {
        "ocean_state": gaussian(streams_of[0], (ENS, C, NY, NX), 1.0, 6.0, ((0, 4), (2, 4), (3, 2))),
        "ocean_mask": draw_ocean_mask(jax.random.fold_in(streams_of[7], 71), 0),
        "dw_weight": gaussian(streams_of[2], (C, KS * KS), (KS * KS) ** -0.5, 0.875, (), jnp.float32),
        "norm_gain": jnp.clip(1.0 + 0.18 * jax.random.normal(streams_of[3], (C,), jnp.float32), 0.1, 1.9),
        "expand_weight": gaussian(streams_of[4], (C, HID), C ** -0.5, 0.4375),
        "reduce_weight": gaussian(streams_of[5], (HID, C), HID ** -0.5, 0.21875),
        "cotangent": gaussian(streams_of[6], (ENS, C, NY, NX), 1.0, 6.0, ((0, 4), (2, 4), (3, 2))),
    }


norm_eps = 1e-06
root_half = 0.7071067811865476
gauss_norm = 0.3989422804014327

def pad_global(field_in):
    margin = KS // 2
    wrapped = jnp.concatenate([field_in[:, :, NX - margin:], field_in, field_in[:, :, :margin]], axis=2)
    north_rows = wrapped[:, NY - margin:, :][:, ::-1, ::-1]
    south_rows = jnp.zeros_like(north_rows)
    return jnp.concatenate([south_rows, wrapped, north_rows], axis=1)

def depthwise(padded, dw_weight, out_rows, out_cols):
    conv_sum = jnp.zeros((padded.shape[0], out_rows, out_cols), jnp.float32)
    for shift_a in range(KS):
        for shift_b in range(KS):
            tap_weight = dw_weight[:, shift_a * KS + shift_b][:, None, None]
            window = padded[:, shift_a:shift_a + out_rows, shift_b:shift_b + out_cols].astype(jnp.float32)
            conv_sum = conv_sum + tap_weight * window
    return conv_sum

def depthwise_grad(d_conv, padded, out_rows, out_cols):
    columns = []
    for shift_a in range(KS):
        for shift_b in range(KS):
            window = padded[:, shift_a:shift_a + out_rows, shift_b:shift_b + out_cols].astype(jnp.float32)
            columns.append(lax.optimization_barrier(jnp.sum(d_conv * window, axis=(1, 2))))
    return jnp.stack(columns, axis=1)

def cell_pass(conv_blk, state_blk, cot_blk, mask_blk, norm_gain, expand_weight, reduce_weight):
    chan_mean = lax.optimization_barrier(jnp.mean(conv_blk, axis=0, keepdims=True))
    centred = conv_blk - chan_mean
    chan_var = lax.optimization_barrier(jnp.mean(centred * centred, axis=0, keepdims=True))
    inv_std = lax.rsqrt(chan_var + norm_eps)
    normed = centred * inv_std
    scaled = (normed * norm_gain[:, None]).astype(jnp.bfloat16)
    pre_act = jnp.dot(expand_weight.T, scaled, preferred_element_type=jnp.float32)
    normal_cdf = 0.5 * (1.0 + lax.erf(pre_act * root_half))
    normal_pdf = jnp.exp(-0.5 * pre_act * pre_act) * gauss_norm
    hidden = (pre_act * normal_cdf).astype(jnp.bfloat16)
    gelu_slope = normal_cdf + pre_act * normal_pdf
    branch = jnp.dot(reduce_weight.T, hidden, preferred_element_type=jnp.float32)
    out_blk = ((state_blk.astype(jnp.float32) + branch) * mask_blk[None, :]).astype(jnp.bfloat16)
    grad_reduce = jnp.dot(hidden, cot_blk.T, preferred_element_type=jnp.float32)
    d_hidden = jnp.dot(reduce_weight, cot_blk, preferred_element_type=jnp.float32)
    d_pre = (d_hidden * gelu_slope).astype(jnp.bfloat16)
    grad_expand = jnp.dot(scaled, d_pre.T, preferred_element_type=jnp.float32)
    d_scaled = jnp.dot(expand_weight, d_pre, preferred_element_type=jnp.float32)
    grad_gain = lax.optimization_barrier(jnp.sum(d_scaled * normed, axis=1))
    d_normed = d_scaled * norm_gain[:, None]
    d_conv = inv_std * (d_normed - lax.optimization_barrier(jnp.mean(d_normed, axis=0, keepdims=True)) - normed * lax.optimization_barrier(jnp.mean(d_normed * normed, axis=0, keepdims=True)))
    return (out_blk, d_conv, grad_expand, grad_reduce, grad_gain)

def member_pass(state_one, cot_one, ocean_mask, dw_weight, norm_gain, expand_weight, reduce_weight):
    mask_bf = ocean_mask.astype(jnp.bfloat16)
    masked = state_one * mask_bf[None]
    padded = pad_global(masked)
    conv_out = depthwise(padded, dw_weight, NY, NX)
    cells_all = NY * NX
    block_count = NY // TH * (NX // TW)
    block_len = cells_all // block_count

    def to_blocks(array_in):
        return array_in.reshape(array_in.shape[0], block_count, block_len).transpose(1, 0, 2)
    conv_blocks = to_blocks(conv_out.reshape(C, cells_all))
    state_blocks = to_blocks(state_one.reshape(C, cells_all))
    cot_blocks = to_blocks((cot_one * mask_bf[None]).reshape(C, cells_all))
    mask_blocks = ocean_mask.astype(jnp.float32).reshape(block_count, block_len)

    def block_step(carry, pieces):
        out_blk, d_conv, grad_expand, grad_reduce, grad_gain = cell_pass(pieces[0], pieces[1], pieces[2], pieces[3], norm_gain, expand_weight, reduce_weight)
        return ((carry[0] + grad_expand, carry[1] + grad_reduce, carry[2] + grad_gain), (out_blk, d_conv))
    start = (jnp.zeros((C, HID), jnp.float32), jnp.zeros((HID, C), jnp.float32), jnp.zeros((C,), jnp.float32))
    totals, stacked = lax.scan(block_step, start, (conv_blocks, state_blocks, cot_blocks, mask_blocks))
    out_full = stacked[0].transpose(1, 0, 2).reshape(C, NY, NX)
    d_conv_full = stacked[1].transpose(1, 0, 2).reshape(C, NY, NX)
    grad_depthwise = depthwise_grad(d_conv_full, padded, NY, NX)
    return (out_full, totals[0], totals[1], totals[2], grad_depthwise)

def reference(ocean_state, ocean_mask, dw_weight, norm_gain, expand_weight, reduce_weight, cotangent):

    def one_member(pair):
        return member_pass(pair[0], pair[1], ocean_mask, dw_weight, norm_gain, expand_weight, reduce_weight)
    results = lax.map(one_member, (ocean_state, cotangent))
    grad_scale = 1.0 / math.sqrt(ENS * NY * NX)
    next_state = results[0]
    grad_expand = lax.optimization_barrier(jnp.sum(results[1], axis=0)) * grad_scale
    grad_reduce = lax.optimization_barrier(jnp.sum(results[2], axis=0)) * grad_scale
    grad_gain = lax.optimization_barrier(jnp.sum(results[3], axis=0)) * grad_scale
    grad_depthwise = lax.optimization_barrier(jnp.sum(results[4], axis=0)) * grad_scale
    return (next_state, grad_depthwise, grad_gain, grad_expand, grad_reduce)
```

```python
import functools
import math

import jax
import jax.numpy as jnp
from jax import lax
from jax.experimental import pallas as pl
from jax.experimental.pallas import tpu as pltpu
from jax.sharding import PartitionSpec as P

KS = 7


norm_eps = 1e-06
root_half = 0.7071067811865476
gauss_norm = 0.3989422804014327


MESH_AXES = ("ens", "lon", "lat")
TILE = 16
LANES = 128


def bits_of(axis, size, first=0):
    return [(axis, 1 << k, 2) for k in range(first, size.bit_length() - 1)]


def make_streams(sizes):
    lead = bits_of("lat", sizes["lat"])[:1]
    groups = [bits_of("lat", sizes["lat"], 1), bits_of("lon", sizes["lon"])]
    groups.append([("ens", 1, sizes["ens"])])
    groups = [[digit for digit in group if digit[2] > 1] for group in groups]
    streams = []
    for turn in range(3):
        order = groups[turn:] + groups[:turn]
        streams.append(lead + [digit for group in order for digit in group])
    return streams


class Reducer:
    def __init__(self, sizes, tiles_used):
        self.streams = make_streams(sizes)
        self.count = math.prod(sizes.values())
        share = -(-tiles_used // len(self.streams))
        self.share = -(-share // self.count) * self.count
        self.tiles = self.share * len(self.streams)
        self.copies = []
        slots = []
        for number, stages in enumerate(self.streams):
            extent = self.share
            place = number * self.share
            for level, (axis, stride, radix) in enumerate(stages):
                extent //= radix
                for turn in range(1, radix):
                    slots.append((number, level, turn, place))
                    place += extent
        self.slots = {(n, v, t): (i, p) for i, (n, v, t, p) in enumerate(slots)}

    def scratch(self):
        n = len(self.slots)
        return [
            pltpu.VMEM((2 * self.tiles, 8, LANES), jnp.float32),
            pltpu.VMEM((self.tiles, TILE, LANES), jnp.bfloat16),
            pltpu.VMEM((self.tiles, TILE, LANES), jnp.bfloat16),
            pltpu.VMEM((self.tiles, TILE, LANES), jnp.bfloat16),
            pltpu.SemaphoreType.DMA((n,)),
            pltpu.SemaphoreType.DMA((n,)),
            pltpu.SemaphoreType.DMA((n,)),
            pltpu.SemaphoreType.DMA((n,)),
        ]

    def bind(self, acc, send, recv, full, ss, rs, sg, rg):
        self.acc, self.send, self.recv, self.full = acc, send, recv, full
        self.ss, self.rs, self.sg, self.rg = ss, rs, sg, rg
        where = {axis: lax.axis_index(axis) for axis in MESH_AXES}
        self.where = where
        self.starts = []
        self.extents = []
        for number, stages in enumerate(self.streams):
            start = number * self.share
            extent = self.share
            starts, extents = [start], [extent]
            for axis, stride, radix in stages:
                extent //= radix
                start = start + lax.rem(lax.div(where[axis], stride), radix) * extent
                starts.append(start)
                extents.append(extent)
            self.starts.append(starts)
            self.extents.append(extents)
        return self

    def peer(self, digit, turn):
        axis, stride, radix = digit
        mine = lax.rem(lax.div(self.where[axis], stride), radix)
        theirs = lax.rem(mine + turn, radix)
        return theirs, {axis: self.where[axis] + (theirs - mine) * stride}

    def peers(self):
        seen = set()
        found = []
        for stages in self.streams:
            for digit in stages:
                for turn in range(1, digit[2]):
                    if (digit, turn) not in seen:
                        seen.add((digit, turn))
                        found.append(self.peer(digit, turn)[1])
        return found

    def scatter_copy(self, number, level, turn):
        digit = self.streams[number][level]
        extent = self.extents[number][level + 1]
        theirs, device = self.peer(digit, turn)
        begin = self.starts[number][level] + theirs * extent
        slot, place = self.slots[number, level, turn]
        copy = pltpu.make_async_remote_copy(
            src_ref=self.send.at[pl.ds(begin, extent)],
            dst_ref=self.recv.at[pl.ds(place, extent)],
            send_sem=self.ss.at[slot],
            recv_sem=self.rs.at[slot],
            device_id=device,
            device_id_type=pl.DeviceIdType.MESH,
        )
        return copy, begin, extent, place

    def scatter_start(self, number, level):
        for turn in range(1, self.streams[number][level][2]):
            copy, begin, extent, _ = self.scatter_copy(number, level, turn)
            piece = self.acc[pl.ds(2 * begin, 2 * extent)].astype(jnp.bfloat16)
            self.send[pl.ds(begin, extent)] = piece.reshape(extent, TILE, LANES)
            copy.start()

    def scatter_finish(self, number, level):
        begin = self.starts[number][level + 1]
        extent = self.extents[number][level + 1]
        total = self.acc[pl.ds(2 * begin, 2 * extent)]
        for turn in range(1, self.streams[number][level][2]):
            copy, _, _, place = self.scatter_copy(number, level, turn)
            copy.wait_recv()
            piece = self.recv[pl.ds(place, extent)].astype(jnp.float32)
            total = total + piece.reshape(2 * extent, 8, LANES)
        self.acc[pl.ds(2 * begin, 2 * extent)] = total

    def gather_copy(self, number, level, turn):
        _, device = self.peer(self.streams[number][level], turn)
        begin = self.starts[number][level + 1]
        extent = self.extents[number][level + 1]
        slot, _ = self.slots[number, level, turn]
        block = self.full.at[pl.ds(begin, extent)]
        return pltpu.make_async_remote_copy(
            src_ref=block,
            dst_ref=block,
            send_sem=self.sg.at[slot],
            recv_sem=self.rg.at[slot],
            device_id=device,
            device_id_type=pl.DeviceIdType.MESH,
        )

    def turns(self, number, level):
        return range(1, self.streams[number][level][2])

    def gather_start(self, number, level):
        for turn in self.turns(number, level):
            self.gather_copy(number, level, turn).start()

    def gather_finish(self, number, level):
        for turn in self.turns(number, level):
            self.gather_copy(number, level, turn).wait_recv()

    def scatter_first(self):
        for number in range(len(self.streams)):
            self.scatter_start(number, 0)

    def run(self):
        numbers = range(len(self.streams))
        depth = len(self.streams[0])
        for level in range(depth):
            for number in numbers:
                self.scatter_finish(number, level)
                if level + 1 < depth:
                    self.scatter_start(number, level + 1)
                else:
                    begin, extent = self.starts[number][-1], self.extents[number][-1]
                    mine = self.acc[pl.ds(2 * begin, 2 * extent)].astype(jnp.bfloat16)
                    self.full[pl.ds(begin, extent)] = mine.reshape(extent, TILE, LANES)
                    self.gather_start(number, level)
        for level in reversed(range(depth)):
            for number in numbers:
                self.gather_finish(number, level)
                if level > 0:
                    self.gather_start(number, level - 1)
        for number in numbers:
            for level in range(depth):
                for turn in self.turns(number, level):
                    self.scatter_copy(number, level, turn)[0].wait_send()
                    self.gather_copy(number, level, turn).wait_send()


def greet(devices):
    barrier = pltpu.get_barrier_semaphore()
    for device in devices:
        pl.semaphore_signal(
            barrier, inc=1, device_id=device, device_id_type=pl.DeviceIdType.MESH
        )
    pl.semaphore_wait(barrier, len(devices))


def pack(acc, lane_tile, row_tile, block):
    rows, width = block.shape
    begin = lane_tile + row_tile
    acc[begin : begin + rows // 8, :, :width] = block.reshape(rows // 8, 8, width)


def reduce_kernel(reducer, scale, expand_ref, reduce_ref, small_ref, expand_out, reduce_out, small_out, *scratch):
    channels, hidden = expand_ref.shape
    eights = channels // 8
    acc, full = scratch[0], scratch[3]
    reducer.bind(*scratch)
    spans = [(low, min(low + LANES, hidden)) for low in range(0, hidden, LANES)]
    acc[...] = jnp.zeros_like(acc)
    for at, (low, high) in enumerate(spans):
        pack(acc, at * 2 * eights, 0, expand_ref[:, low:high] * scale)
        pack(acc, at * 2 * eights, eights, reduce_ref[:, low:high] * scale)
    pack(acc, len(spans) * 2 * eights, 0, small_ref[...] * scale)
    greet(reducer.peers())
    reducer.scatter_first()
    reducer.run()
    for at, (low, high) in enumerate(spans):
        both = full[at * eights : (at + 1) * eights].astype(jnp.float32)
        both = both.reshape(2 * channels, LANES)
        expand_out[:, low:high] = both[:channels, : high - low]
        reduce_out[low:high, :] = both[channels:].T[: high - low, :]
    begin = len(spans) * eights
    rest = full[begin : begin + -(-eights // 2)].astype(jnp.float32).reshape(-1, LANES)
    small_out[...] = rest[:channels, : small_out.shape[1]]


def all_reduce(sizes, scale, grad_expand, grad_reduce_t, small):
    channels, hidden = grad_expand.shape
    eights = channels // 8
    tiles = -(-hidden // LANES) * eights + -(-eights // 2)
    reducer = Reducer(sizes, tiles)
    vmem = pl.BlockSpec(memory_space=pltpu.VMEM)
    return pl.pallas_call(
        functools.partial(reduce_kernel, reducer, scale),
        out_shape=(
            jax.ShapeDtypeStruct((channels, hidden), jnp.float32),
            jax.ShapeDtypeStruct((hidden, channels), jnp.float32),
            jax.ShapeDtypeStruct(small.shape, jnp.float32),
        ),
        in_specs=[vmem] * 3,
        out_specs=[vmem] * 3,
        scratch_shapes=reducer.scratch(),
        compiler_params=pltpu.CompilerParams(
            collective_id=0, has_side_effects=True, vmem_limit_bytes=56 * 1024 * 1024
        ),
    )(grad_expand, grad_reduce_t, small)


def with_halo(cells, sides, width):
    for axis, dim in sides:
        count = lax.axis_size(axis)
        head = lax.slice_in_dim(cells, 0, width, axis=dim)
        tail = lax.slice_in_dim(cells, cells.shape[dim] - width, cells.shape[dim], axis=dim)
        cells = jnp.concatenate(
            [
                lax.ppermute(tail, axis, [(i, (i + 1) % count) for i in range(count)]),
                cells,
                lax.ppermute(head, axis, [((i + 1) % count, i) for i in range(count)]),
            ],
            axis=dim,
        )
    return cells


def swapped(array, axis, stride):
    return lax.ppermute(array, axis, [(i, i ^ 1 << stride) for i in range(lax.axis_size(axis))])


def depthwise(padded, dw_weight, out_rows, out_cols):
    conv_sum = jnp.zeros((padded.shape[0], out_rows, out_cols), jnp.float32)
    for shift_a in range(KS):
        for shift_b in range(KS):
            tap_weight = dw_weight[:, shift_a * KS + shift_b][:, None, None]
            window = padded[:, shift_a : shift_a + out_rows, shift_b : shift_b + out_cols].astype(
                jnp.float32
            )
            conv_sum = conv_sum + tap_weight * window
    return conv_sum


def depthwise_grad(d_conv, padded, out_rows, out_cols):
    columns = []
    for shift_a in range(KS):
        for shift_b in range(KS):
            window = padded[:, shift_a : shift_a + out_rows, shift_b : shift_b + out_cols].astype(
                jnp.float32
            )
            columns.append(jnp.sum(d_conv * window, axis=(1, 2)))
    return jnp.stack(columns, axis=1)


def cell_pass(conv_blk, state_blk, cot_blk, mask_blk, norm_gain, expand_weight, reduce_weight):
    chan_mean = jnp.mean(conv_blk, axis=0, keepdims=True)
    centred = conv_blk - chan_mean
    chan_var = jnp.mean(centred * centred, axis=0, keepdims=True)
    inv_std = lax.rsqrt(chan_var + norm_eps)
    normed = centred * inv_std
    scaled = (normed * norm_gain[:, None]).astype(jnp.bfloat16)
    pre_act = jnp.dot(expand_weight.T, scaled, preferred_element_type=jnp.float32)
    normal_cdf = 0.5 * (1.0 + lax.erf(pre_act * root_half))
    normal_pdf = jnp.exp(-0.5 * pre_act * pre_act) * gauss_norm
    hidden = (pre_act * normal_cdf).astype(jnp.bfloat16)
    gelu_slope = normal_cdf + pre_act * normal_pdf
    branch = jnp.dot(reduce_weight.T, hidden, preferred_element_type=jnp.float32)
    out_blk = ((state_blk.astype(jnp.float32) + branch) * mask_blk[None, :]).astype(jnp.bfloat16)
    grad_reduce = jnp.dot(cot_blk, hidden.T, preferred_element_type=jnp.float32)
    d_hidden = jnp.dot(reduce_weight, cot_blk, preferred_element_type=jnp.float32)
    d_pre = (d_hidden * gelu_slope).astype(jnp.bfloat16)
    grad_expand = jnp.dot(scaled, d_pre.T, preferred_element_type=jnp.float32)
    d_scaled = jnp.dot(expand_weight, d_pre, preferred_element_type=jnp.float32)
    grad_gain = jnp.sum(d_scaled * normed, axis=1)
    d_normed = d_scaled * norm_gain[:, None]
    d_conv = inv_std * (
        d_normed
        - jnp.mean(d_normed, axis=0, keepdims=True)
        - normed * jnp.mean(d_normed * normed, axis=0, keepdims=True)
    )
    return (out_blk, d_conv, grad_expand, grad_reduce, grad_gain)


def body(ocean_state, ocean_mask, dw_weight, norm_gain, expand_weight, reduce_weight, cotangent):
    state_tile = ocean_state[0]
    channels = state_tile.shape[0]
    tile_rows = state_tile.shape[1]
    tile_cols = state_tile.shape[2]
    margin = KS // 2
    mask_bf = ocean_mask.astype(jnp.bfloat16)
    masked = state_tile * mask_bf[None]
    padded = with_halo(masked, (("lon", 2), ("lat", 1)), margin)
    lat_now = lax.axis_index("lat")
    lat_count = lax.axis_size("lat")
    lon_count = lax.axis_size("lon")
    top_strip = padded[:, tile_rows : tile_rows + margin, :][:, ::-1, ::-1]
    mirrored = top_strip
    for bit_number in range(lon_count.bit_length() - 1):
        mirrored = swapped(mirrored, "lon", bit_number)
    north_rows = jnp.where(lat_now == lat_count - 1, mirrored, padded[:, tile_rows + margin :, :])
    south_rows = jnp.where(lat_now == 0, jnp.zeros_like(top_strip), padded[:, :margin, :])
    padded = jnp.concatenate(
        [south_rows, padded[:, margin : tile_rows + margin, :], north_rows], axis=1
    )
    conv_out = depthwise(padded, dw_weight, tile_rows, tile_cols)
    cell_count = tile_rows * tile_cols
    cot_masked = (cotangent[0] * mask_bf[None]).reshape(channels, cell_count)
    out_flat, d_conv, grad_expand, grad_reduce, grad_gain = cell_pass(
        conv_out.reshape(channels, cell_count),
        state_tile.reshape(channels, cell_count),
        cot_masked,
        ocean_mask.astype(jnp.float32).reshape(cell_count),
        norm_gain,
        expand_weight,
        reduce_weight,
    )
    grad_depthwise = depthwise_grad(
        d_conv.reshape(channels, tile_rows, tile_cols), padded, tile_rows, tile_cols
    )
    grad_scale = 1.0 / math.sqrt(lax.axis_size("ens") * lat_count * lon_count * cell_count)
    sizes = {axis: lax.axis_size(axis) for axis in MESH_AXES}
    small = jnp.concatenate([grad_depthwise, grad_gain[:, None]], axis=1)
    grad_expand, grad_reduce, small = all_reduce(
        sizes, grad_scale, grad_expand, grad_reduce, small
    )
    grad_depthwise, grad_gain = small[:, :-1], small[:, -1]
    next_state = out_flat.reshape(channels, tile_rows, tile_cols)[None]
    return (next_state, grad_depthwise, grad_gain, grad_expand, grad_reduce)


def solution(mesh):
    return jax.shard_map(
        body,
        mesh=mesh,
        in_specs=(
            P("ens", None, "lat", "lon"),
            P("lat", "lon"),
            P(),
            P(),
            P(),
            P(),
            P("ens", None, "lat", "lon"),
        ),
        out_specs=(P("ens", None, "lat", "lon"), P(), P(), P(), P()),
        check_vma=False,
    )
```

```python
import functools
import math

import jax
import jax.numpy as jnp
from jax import lax
from jax.experimental import pallas as pl
from jax.experimental.pallas import tpu as pltpu
from jax.sharding import PartitionSpec as P

KS = 7


norm_eps = 1e-06
root_half = 0.7071067811865476
gauss_norm = 0.3989422804014327


MESH_AXES = ("ens", "lon", "lat")
TILE = 16
LANES = 128


def bits_of(axis, size, first=0):
    return [(axis, 1 << k, 2) for k in range(first, size.bit_length() - 1)]


def big_streams(sizes):
    lead = bits_of("lat", sizes["lat"])[:1]
    groups = [bits_of("lat", sizes["lat"], 1), bits_of("lon", sizes["lon"])]
    groups.append([("ens", 1, sizes["ens"])])
    groups = [[digit for digit in group if digit[2] > 1] for group in groups]
    streams = []
    for turn in range(3):
        order = groups[turn:] + groups[:turn]
        streams.append(lead + [digit for group in order for digit in group])
    return streams


def small_streams(sizes):
    stages = []
    for axis in ("lat", "lon", "ens"):
        whole = [(axis, 1, sizes[axis])] if sizes[axis] <= 4 else bits_of(axis, sizes[axis])
        stages += [digit for digit in whole if digit[2] > 1]
    return [stages]


class Reducer:
    def __init__(self, sizes, streams, tiles_used):
        self.streams = streams
        self.count = math.prod(sizes.values())
        share = -(-tiles_used // len(self.streams))
        self.share = -(-share // self.count) * self.count
        self.tiles = self.share * len(self.streams)
        slots = []
        for number, stages in enumerate(self.streams):
            extent = self.share
            place = number * self.share
            for level, (axis, stride, radix) in enumerate(stages):
                extent //= radix
                for turn in range(1, radix):
                    slots.append((number, level, turn, place))
                    place += extent
        self.slots = {(n, v, t): (i, p) for i, (n, v, t, p) in enumerate(slots)}

    def scratch(self):
        n = len(self.slots)
        return [
            pltpu.VMEM((2 * self.tiles, 8, LANES), jnp.float32),
            pltpu.VMEM((self.tiles, TILE, LANES), jnp.bfloat16),
            pltpu.VMEM((self.tiles, TILE, LANES), jnp.bfloat16),
            pltpu.VMEM((self.tiles, TILE, LANES), jnp.bfloat16),
            pltpu.SemaphoreType.DMA((n,)),
            pltpu.SemaphoreType.DMA((n,)),
            pltpu.SemaphoreType.DMA((n,)),
            pltpu.SemaphoreType.DMA((n,)),
        ]

    def bind(self, acc, send, recv, full, ss, rs, sg, rg):
        self.acc, self.send, self.recv, self.full = acc, send, recv, full
        self.ss, self.rs, self.sg, self.rg = ss, rs, sg, rg
        where = {axis: lax.axis_index(axis) for axis in MESH_AXES}
        self.where = where
        self.starts = []
        self.extents = []
        for number, stages in enumerate(self.streams):
            start = number * self.share
            extent = self.share
            starts, extents = [start], [extent]
            for axis, stride, radix in stages:
                extent //= radix
                start = start + lax.rem(lax.div(where[axis], stride), radix) * extent
                starts.append(start)
                extents.append(extent)
            self.starts.append(starts)
            self.extents.append(extents)
        return self

    def peer(self, digit, turn):
        axis, stride, radix = digit
        mine = lax.rem(lax.div(self.where[axis], stride), radix)
        theirs = lax.rem(mine + turn, radix)
        return theirs, {axis: self.where[axis] + (theirs - mine) * stride}

    def peers(self):
        seen = set()
        found = []
        for stages in self.streams:
            for digit in stages:
                for turn in range(1, digit[2]):
                    if (digit, turn) not in seen:
                        seen.add((digit, turn))
                        found.append(self.peer(digit, turn)[1])
        return found

    def scatter_copy(self, number, level, turn):
        digit = self.streams[number][level]
        extent = self.extents[number][level + 1]
        theirs, device = self.peer(digit, turn)
        begin = self.starts[number][level] + theirs * extent
        slot, place = self.slots[number, level, turn]
        copy = pltpu.make_async_remote_copy(
            src_ref=self.send.at[pl.ds(begin, extent)],
            dst_ref=self.recv.at[pl.ds(place, extent)],
            send_sem=self.ss.at[slot],
            recv_sem=self.rs.at[slot],
            device_id=device,
            device_id_type=pl.DeviceIdType.MESH,
        )
        return copy, begin, extent, place

    def scatter_start(self, number, level):
        for turn in range(1, self.streams[number][level][2]):
            copy, begin, extent, _ = self.scatter_copy(number, level, turn)
            piece = self.acc[pl.ds(2 * begin, 2 * extent)].astype(jnp.bfloat16)
            self.send[pl.ds(begin, extent)] = piece.reshape(extent, TILE, LANES)
            copy.start()

    def scatter_finish(self, number, level):
        begin = self.starts[number][level + 1]
        extent = self.extents[number][level + 1]
        total = self.acc[pl.ds(2 * begin, 2 * extent)]
        for turn in range(1, self.streams[number][level][2]):
            copy, _, _, place = self.scatter_copy(number, level, turn)
            copy.wait_recv()
            piece = self.recv[pl.ds(place, extent)].astype(jnp.float32)
            total = total + piece.reshape(2 * extent, 8, LANES)
        self.acc[pl.ds(2 * begin, 2 * extent)] = total

    def gather_copy(self, number, level, turn):
        _, device = self.peer(self.streams[number][level], turn)
        begin = self.starts[number][level + 1]
        extent = self.extents[number][level + 1]
        slot, _ = self.slots[number, level, turn]
        block = self.full.at[pl.ds(begin, extent)]
        return pltpu.make_async_remote_copy(
            src_ref=block,
            dst_ref=block,
            send_sem=self.sg.at[slot],
            recv_sem=self.rg.at[slot],
            device_id=device,
            device_id_type=pl.DeviceIdType.MESH,
        )

    def turns(self, number, level):
        return range(1, self.streams[number][level][2])

    def gather_start(self, number, level):
        for turn in self.turns(number, level):
            self.gather_copy(number, level, turn).start()

    def gather_finish(self, number, level):
        for turn in self.turns(number, level):
            self.gather_copy(number, level, turn).wait_recv()

    def clear(self):
        self.acc[...] = jnp.zeros_like(self.acc)

    def steps(self):
        numbers = range(len(self.streams))
        depth = len(self.streams[0])
        for number in numbers:
            self.scatter_start(number, 0)
        yield True
        for level in range(depth):
            for number in numbers:
                self.scatter_finish(number, level)
                if level + 1 < depth:
                    self.scatter_start(number, level + 1)
                else:
                    begin, extent = self.starts[number][-1], self.extents[number][-1]
                    mine = self.acc[pl.ds(2 * begin, 2 * extent)].astype(jnp.bfloat16)
                    self.full[pl.ds(begin, extent)] = mine.reshape(extent, TILE, LANES)
                    self.gather_start(number, level)
            yield True
        for level in reversed(range(depth)):
            for number in numbers:
                self.gather_finish(number, level)
                if level > 0:
                    self.gather_start(number, level - 1)
            yield True
        for number in numbers:
            for level in range(depth):
                for turn in self.turns(number, level):
                    self.scatter_copy(number, level, turn)[0].wait_send()
                    self.gather_copy(number, level, turn).wait_send()


def pack(acc, lane_tile, row_tile, block):
    rows, width = block.shape
    begin = lane_tile + row_tile
    acc[begin : begin + rows // 8, :, :width] = block.reshape(rows // 8, 8, width)


def with_halo(cells, sides, width):
    for axis, dim in sides:
        count = lax.axis_size(axis)
        head = lax.slice_in_dim(cells, 0, width, axis=dim)
        tail = lax.slice_in_dim(cells, cells.shape[dim] - width, cells.shape[dim], axis=dim)
        cells = jnp.concatenate(
            [
                lax.ppermute(tail, axis, [(i, (i + 1) % count) for i in range(count)]),
                cells,
                lax.ppermute(head, axis, [((i + 1) % count, i) for i in range(count)]),
            ],
            axis=dim,
        )
    return cells


def swapped(array, axis, stride):
    return lax.ppermute(array, axis, [(i, i ^ 1 << stride) for i in range(lax.axis_size(axis))])


def lane_spans(width):
    return [(low, min(low + LANES, width)) for low in range(0, width, LANES)]


def window(main, edge, lane, shift):
    width = main.shape[1]
    if shift == 0:
        return main
    outside = lane < shift if shift > 0 else lane >= width + shift
    return pltpu.roll(jnp.where(outside, edge, main), (-shift) % width, 1)


def block_kernel(
    big,
    small,
    scale,
    main_ref,
    edge_ref,
    cot_ref,
    mask_ref,
    dw_ref,
    gain_ref,
    expand_ref,
    reduce_ref,
    state_out,
    expand_out,
    reduce_out,
    small_out,
    expand_t,
    reduce_t,
    conv,
    scaled_all,
    hidden_all,
    d_pre_all,
    gain_sum,
    *scratch,
):
    channels, hidden_units = expand_ref.shape
    eights = channels // 8
    margin = KS // 2
    tile_rows = main_ref.shape[0] - 2 * margin
    width = main_ref.shape[2]
    spans = lane_spans(hidden_units)
    big.bind(*scratch[:8])
    small.bind(*scratch[8:])
    peers = big.peers() + small.peers()
    barrier_count = len(peers)
    barrier = pltpu.get_barrier_semaphore()
    for device in peers:
        pl.semaphore_signal(
            barrier, inc=1, device_id=device, device_id_type=pl.DeviceIdType.MESH
        )
    big.clear()
    small.clear()
    gain_sum[...] = jnp.zeros_like(gain_sum)
    for low, high in spans:
        piece = expand_ref[:, low:high].astype(jnp.float32).T
        expand_t[low:high, :] = piece.astype(jnp.bfloat16)
        piece = reduce_ref[low:high, :].astype(jnp.float32).T
        reduce_t[:, low:high] = piece.astype(jnp.bfloat16)
    lane = lax.broadcasted_iota(jnp.int32, (8, width), 1)

    def conv_step(step, carry):
        rows = pl.ds(pl.multiple_of(step * 8, 8), 8)
        taps = dw_ref[rows, :]
        sums = [jnp.zeros((8, width), jnp.float32) for _ in range(tile_rows)]
        for shift_b in range(KS):
            weights = [
                jnp.broadcast_to(taps[:, a * KS + shift_b : a * KS + shift_b + 1], (8, width))
                for a in range(KS)
            ]
            for row in range(tile_rows + 2 * margin):
                cells = window(main_ref[row, rows, :], edge_ref[row, rows, :], lane, shift_b - margin)
                for shift_a in range(KS):
                    if 0 <= row - shift_a < tile_rows:
                        sums[row - shift_a] = sums[row - shift_a] + weights[shift_a] * cells
        for row in range(tile_rows):
            conv[rows, row * width : (row + 1) * width] = sums[row]
        return carry

    lax.fori_loop(0, eights, conv_step, 0)

    gain = gain_ref[...]
    block_rows = 2
    block = block_rows * width

    def cell_step(step, carry):
        cells = pl.ds(pl.multiple_of(step * block, block), block)
        conv_blk = conv[:, cells]
        centred = conv_blk - jnp.mean(conv_blk, axis=0, keepdims=True)
        inv_std = lax.rsqrt(jnp.mean(centred * centred, axis=0, keepdims=True) + norm_eps)
        normed = centred * inv_std
        scaled = (normed * gain).astype(jnp.bfloat16)
        scaled_all[:, cells] = scaled
        pre_act = jnp.dot(expand_t[...], scaled, preferred_element_type=jnp.float32)
        normal_cdf = 0.5 * (1.0 + lax.erf(pre_act * root_half))
        normal_pdf = jnp.exp(-0.5 * pre_act * pre_act) * gauss_norm
        hidden = (pre_act * normal_cdf).astype(jnp.bfloat16)
        gelu_slope = normal_cdf + pre_act * normal_pdf
        d_hidden = jnp.dot(reduce_ref[...], cot_ref[:, cells], preferred_element_type=jnp.float32)
        d_pre = (d_hidden * gelu_slope).astype(jnp.bfloat16)
        hidden_all[:, cells] = hidden
        d_pre_all[:, cells] = d_pre
        branch = jnp.dot(reduce_t[...], hidden, preferred_element_type=jnp.float32)
        for part in range(block_rows):
            row = step * block_rows + part
            at = pl.ds(pl.multiple_of(row * width, width), width)
            total = main_ref[margin + row] + branch[:, part * width : (part + 1) * width]
            state_out[:, at] = (total * mask_ref[:, at]).astype(jnp.bfloat16)
        d_scaled = jnp.dot(expand_ref[...], d_pre, preferred_element_type=jnp.float32)
        product = d_scaled * normed
        for part in range(block_rows):
            gain_sum[...] += product[:, part * width : (part + 1) * width]
        d_normed = d_scaled * gain
        mean_one = jnp.mean(d_normed, axis=0, keepdims=True)
        mean_two = jnp.mean(d_normed * normed, axis=0, keepdims=True)
        conv[:, cells] = inv_std * (d_normed - mean_one - normed * mean_two)
        return carry

    lax.fori_loop(0, tile_rows // block_rows, cell_step, 0)

    over_cells = (((1,), (1,)), ((), ()))
    for at, (low, high) in enumerate(spans):
        grad = lax.dot_general(
            scaled_all[...], d_pre_all[low:high, :], over_cells, preferred_element_type=jnp.float32
        )
        pack(big.acc, at * 2 * eights, 0, grad * scale)
        grad = lax.dot_general(
            cot_ref[...], hidden_all[low:high, :], over_cells, preferred_element_type=jnp.float32
        )
        pack(big.acc, at * 2 * eights, eights, grad * scale)

    def depthwise_step(step, carry):
        rows = pl.ds(pl.multiple_of(step * 8, 8), 8)
        d_conv = [conv[rows, row * width : (row + 1) * width] for row in range(tile_rows)]
        line = jnp.sum(gain_sum[rows, :], axis=1, keepdims=True)
        line = jnp.where(lane == KS * KS, line, 0.0)
        for shift_b in range(KS):
            sums = [jnp.zeros((8, width), jnp.float32) for _ in range(KS)]
            for row in range(tile_rows + 2 * margin):
                cells = window(main_ref[row, rows, :], edge_ref[row, rows, :], lane, shift_b - margin)
                for shift_a in range(KS):
                    if 0 <= row - shift_a < tile_rows:
                        sums[shift_a] = sums[shift_a] + d_conv[row - shift_a] * cells
            for shift_a in range(KS):
                total = jnp.sum(sums[shift_a], axis=1, keepdims=True)
                line = jnp.where(lane == shift_a * KS + shift_b, total, line)
        small.acc[pl.ds(step, 1)] = (line[:, :LANES] * scale).reshape(1, 8, LANES)
        return carry

    pl.semaphore_wait(barrier, barrier_count)
    ahead, behind = big.steps(), small.steps()
    next(ahead)
    lax.fori_loop(0, eights // 2, depthwise_step, 0)
    next(ahead)
    lax.fori_loop(eights // 2, eights, depthwise_step, 0)
    running = [behind, ahead]
    while running:
        running = [one for one in running if next(one, None) is not None]

    for at, (low, high) in enumerate(spans):
        both = big.full[at * eights : (at + 1) * eights].astype(jnp.float32)
        both = both.reshape(2 * channels, LANES)
        expand_out[:, low:high] = both[:channels, : high - low]
        reduce_out[low:high, :] = both[channels:].T[: high - low, :]
    rest = small.full[: -(-eights // 2)].astype(jnp.float32).reshape(-1, LANES)
    small_out[...] = rest[:channels, : small_out.shape[1]]


def block_call(sizes, scale, main, edge, cot, mask, dw_weight, norm_gain, expand_weight, reduce_weight):
    channels, hidden = expand_weight.shape
    cells = cot.shape[1]
    eights = channels // 8
    big = Reducer(sizes, big_streams(sizes), -(-hidden // LANES) * eights)
    small = Reducer(sizes, small_streams(sizes), -(-eights // 2))
    vmem = pl.BlockSpec(memory_space=pltpu.VMEM)
    return pl.pallas_call(
        functools.partial(block_kernel, big, small, scale),
        out_shape=(
            jax.ShapeDtypeStruct((channels, cells), jnp.bfloat16),
            jax.ShapeDtypeStruct((channels, hidden), jnp.float32),
            jax.ShapeDtypeStruct((hidden, channels), jnp.float32),
            jax.ShapeDtypeStruct((channels, KS * KS + 1), jnp.float32),
        ),
        in_specs=[vmem] * 8,
        out_specs=[vmem] * 4,
        scratch_shapes=[
            pltpu.VMEM((hidden, channels), jnp.bfloat16),
            pltpu.VMEM((channels, hidden), jnp.bfloat16),
            pltpu.VMEM((channels, cells), jnp.float32),
            pltpu.VMEM((channels, cells), jnp.bfloat16),
            pltpu.VMEM((hidden, cells), jnp.bfloat16),
            pltpu.VMEM((hidden, cells), jnp.bfloat16),
            pltpu.VMEM((channels, main.shape[2]), jnp.float32),
        ]
        + big.scratch()
        + small.scratch(),
        compiler_params=pltpu.CompilerParams(
            collective_id=0, has_side_effects=True, vmem_limit_bytes=60 * 1024 * 1024
        ),
    )(main, edge, cot, mask, dw_weight, norm_gain[:, None], expand_weight, reduce_weight)


def body(ocean_state, ocean_mask, dw_weight, norm_gain, expand_weight, reduce_weight, cotangent):
    state_tile = ocean_state[0]
    channels, tile_rows, tile_cols = state_tile.shape
    margin = KS // 2
    mask_bf = ocean_mask.astype(jnp.bfloat16)
    masked = state_tile * mask_bf[None]
    padded = with_halo(masked, (("lon", 2), ("lat", 1)), margin)
    lat_now = lax.axis_index("lat")
    lat_count = lax.axis_size("lat")
    lon_count = lax.axis_size("lon")
    top_strip = padded[:, tile_rows : tile_rows + margin, :][:, ::-1, ::-1]
    mirrored = top_strip
    for bit_number in range(lon_count.bit_length() - 1):
        mirrored = swapped(mirrored, "lon", bit_number)
    north_rows = jnp.where(lat_now == lat_count - 1, mirrored, padded[:, tile_rows + margin :, :])
    south_rows = jnp.where(lat_now == 0, jnp.zeros_like(top_strip), padded[:, :margin, :])
    padded = jnp.concatenate(
        [south_rows, padded[:, margin : tile_rows + margin, :], north_rows], axis=1
    )
    padded = padded.transpose(1, 0, 2).astype(jnp.float32)
    main = padded[:, :, margin : margin + tile_cols]
    edge = jnp.concatenate(
        [
            padded[:, :, margin + tile_cols :],
            jnp.zeros(main.shape[:2] + (tile_cols - 2 * margin,), jnp.float32),
            padded[:, :, :margin],
        ],
        axis=2,
    )
    cell_count = tile_rows * tile_cols
    cot_masked = (cotangent[0] * mask_bf[None]).reshape(channels, cell_count)
    grad_scale = 1.0 / math.sqrt(lax.axis_size("ens") * lat_count * lon_count * cell_count)
    sizes = {axis: lax.axis_size(axis) for axis in MESH_AXES}
    out_flat, grad_expand, grad_reduce, small = block_call(
        sizes,
        grad_scale,
        main,
        edge,
        cot_masked,
        ocean_mask.astype(jnp.float32).reshape(1, cell_count),
        dw_weight,
        norm_gain,
        expand_weight,
        reduce_weight,
    )
    next_state = out_flat.reshape(channels, tile_rows, tile_cols)[None]
    return (next_state, small[:, :-1], small[:, -1], grad_expand, grad_reduce)


def solution(mesh):
    return jax.shard_map(
        body,
        mesh=mesh,
        in_specs=(
            P("ens", None, "lat", "lon"),
            P("lat", "lon"),
            P(),
            P(),
            P(),
            P(),
            P("ens", None, "lat", "lon"),
        ),
        out_specs=(P("ens", None, "lat", "lon"), P(), P(), P(), P()),
        check_vma=False,
    )
```

```python
import functools
import math

import jax
import jax.numpy as jnp
from jax import lax
from jax.experimental import pallas as pl
from jax.experimental.pallas import tpu as pltpu
from jax.sharding import PartitionSpec as P

KS = 7


norm_eps = 1e-06
root_half = 0.7071067811865476
gauss_norm = 0.3989422804014327


MESH_AXES = ("ens", "lon", "lat")
TILE = 16
LANES = 128


def bits_of(axis, size, first=0):
    return [(axis, 1 << k, 2) for k in range(first, size.bit_length() - 1)]


def big_streams(sizes):
    lead = bits_of("lat", sizes["lat"])[:1]
    groups = [bits_of("lat", sizes["lat"], 1), bits_of("lon", sizes["lon"])]
    groups.append([("ens", 1, sizes["ens"])])
    groups = [[digit for digit in group if digit[2] > 1] for group in groups]
    streams = []
    for turn in range(3):
        order = groups[turn:] + groups[:turn]
        streams.append(lead + [digit for group in order for digit in group])
    return streams


def small_streams(sizes):
    stages = []
    for axis in ("lat", "lon", "ens"):
        whole = [(axis, 1, sizes[axis])] if sizes[axis] <= 4 else bits_of(axis, sizes[axis])
        stages += [digit for digit in whole if digit[2] > 1]
    return [stages]


class Reducer:
    def __init__(self, sizes, streams, tiles_used):
        self.streams = streams
        self.count = math.prod(sizes.values())
        share = -(-tiles_used // len(self.streams))
        self.share = -(-share // self.count) * self.count
        self.tiles = self.share * len(self.streams)
        slots = []
        for number, stages in enumerate(self.streams):
            extent = self.share
            place = number * self.share
            for level, (axis, stride, radix) in enumerate(stages):
                extent //= radix
                for turn in range(1, radix):
                    slots.append((number, level, turn, place))
                    place += extent
        self.slots = {(n, v, t): (i, p) for i, (n, v, t, p) in enumerate(slots)}

    def scratch(self):
        n = len(self.slots)
        return [
            pltpu.VMEM((2 * self.tiles, 8, LANES), jnp.float32),
            pltpu.VMEM((self.tiles, TILE, LANES), jnp.bfloat16),
            pltpu.VMEM((self.tiles, TILE, LANES), jnp.bfloat16),
            pltpu.VMEM((self.tiles, TILE, LANES), jnp.bfloat16),
            pltpu.SemaphoreType.DMA((n,)),
            pltpu.SemaphoreType.DMA((n,)),
            pltpu.SemaphoreType.DMA((n,)),
            pltpu.SemaphoreType.DMA((n,)),
        ]

    def bind(self, acc, send, recv, full, ss, rs, sg, rg):
        self.acc, self.send, self.recv, self.full = acc, send, recv, full
        self.ss, self.rs, self.sg, self.rg = ss, rs, sg, rg
        where = {axis: lax.axis_index(axis) for axis in MESH_AXES}
        self.where = where
        self.starts = []
        self.extents = []
        for number, stages in enumerate(self.streams):
            start = number * self.share
            extent = self.share
            starts, extents = [start], [extent]
            for axis, stride, radix in stages:
                extent //= radix
                start = start + lax.rem(lax.div(where[axis], stride), radix) * extent
                starts.append(start)
                extents.append(extent)
            self.starts.append(starts)
            self.extents.append(extents)
        return self

    def peer(self, digit, turn):
        axis, stride, radix = digit
        mine = lax.rem(lax.div(self.where[axis], stride), radix)
        theirs = lax.rem(mine + turn, radix)
        return theirs, {axis: self.where[axis] + (theirs - mine) * stride}

    def peers(self):
        seen = set()
        found = []
        for stages in self.streams:
            for digit in stages:
                for turn in range(1, digit[2]):
                    if (digit, turn) not in seen:
                        seen.add((digit, turn))
                        found.append(self.peer(digit, turn)[1])
        return found

    def scatter_copy(self, number, level, turn):
        digit = self.streams[number][level]
        extent = self.extents[number][level + 1]
        theirs, device = self.peer(digit, turn)
        begin = self.starts[number][level] + theirs * extent
        slot, place = self.slots[number, level, turn]
        copy = pltpu.make_async_remote_copy(
            src_ref=self.send.at[pl.ds(begin, extent)],
            dst_ref=self.recv.at[pl.ds(place, extent)],
            send_sem=self.ss.at[slot],
            recv_sem=self.rs.at[slot],
            device_id=device,
            device_id_type=pl.DeviceIdType.MESH,
        )
        return copy, begin, extent, place

    def scatter_start(self, number, level):
        for turn in range(1, self.streams[number][level][2]):
            copy, begin, extent, _ = self.scatter_copy(number, level, turn)
            piece = self.acc[pl.ds(2 * begin, 2 * extent)].astype(jnp.bfloat16)
            self.send[pl.ds(begin, extent)] = piece.reshape(extent, TILE, LANES)
            copy.start()

    def scatter_finish(self, number, level):
        begin = self.starts[number][level + 1]
        extent = self.extents[number][level + 1]
        total = self.acc[pl.ds(2 * begin, 2 * extent)]
        for turn in range(1, self.streams[number][level][2]):
            copy, _, _, place = self.scatter_copy(number, level, turn)
            copy.wait_recv()
            piece = self.recv[pl.ds(place, extent)].astype(jnp.float32)
            total = total + piece.reshape(2 * extent, 8, LANES)
        self.acc[pl.ds(2 * begin, 2 * extent)] = total

    def gather_copy(self, number, level, turn):
        _, device = self.peer(self.streams[number][level], turn)
        begin = self.starts[number][level + 1]
        extent = self.extents[number][level + 1]
        slot, _ = self.slots[number, level, turn]
        block = self.full.at[pl.ds(begin, extent)]
        return pltpu.make_async_remote_copy(
            src_ref=block,
            dst_ref=block,
            send_sem=self.sg.at[slot],
            recv_sem=self.rg.at[slot],
            device_id=device,
            device_id_type=pl.DeviceIdType.MESH,
        )

    def turns(self, number, level):
        return range(1, self.streams[number][level][2])

    def gather_start(self, number, level):
        for turn in self.turns(number, level):
            self.gather_copy(number, level, turn).start()

    def gather_finish(self, number, level):
        for turn in self.turns(number, level):
            self.gather_copy(number, level, turn).wait_recv()

    def clear(self):
        self.acc[...] = jnp.zeros_like(self.acc)

    def steps(self):
        numbers = range(len(self.streams))
        depth = len(self.streams[0])
        for number in numbers:
            self.scatter_start(number, 0)
        yield True
        for level in range(depth):
            for number in numbers:
                self.scatter_finish(number, level)
                if level + 1 < depth:
                    self.scatter_start(number, level + 1)
                else:
                    begin, extent = self.starts[number][-1], self.extents[number][-1]
                    mine = self.acc[pl.ds(2 * begin, 2 * extent)].astype(jnp.bfloat16)
                    self.full[pl.ds(begin, extent)] = mine.reshape(extent, TILE, LANES)
                    self.gather_start(number, level)
            yield True
        for level in reversed(range(depth)):
            for number in numbers:
                self.gather_finish(number, level)
                if level > 0:
                    self.gather_start(number, level - 1)
            yield True
        for number in numbers:
            for level in range(depth):
                for turn in self.turns(number, level):
                    self.scatter_copy(number, level, turn)[0].wait_send()
                    self.gather_copy(number, level, turn).wait_send()


def pack(acc, lane_tile, row_tile, block):
    rows, width = block.shape
    begin = lane_tile + row_tile
    acc[begin : begin + rows // 8, :, :width] = block.reshape(rows // 8, 8, width)


def lane_spans(width):
    return [(low, min(low + LANES, width)) for low in range(0, width, LANES)]


def window(main, edge, lane, shift):
    width = main.shape[1]
    if shift == 0:
        return main
    outside = lane < shift if shift > 0 else lane >= width + shift
    return pltpu.roll(jnp.where(outside, edge, main), (-shift) % width, 1)


class Halo:
    def __init__(self, sizes, margin, rows, channels, width):
        self.sizes, self.margin, self.rows = sizes, margin, rows
        self.channels, self.width = channels, width
        self.pitch = width // rows

    def scratch(self):
        packed = (self.channels, self.width)
        return [
            pltpu.VMEM(packed, jnp.bfloat16),
            pltpu.VMEM((2,) + packed, jnp.bfloat16),
            pltpu.VMEM(packed, jnp.bfloat16),
            pltpu.VMEM((2,) + packed, jnp.bfloat16),
            pltpu.VMEM((2, self.margin) + packed, jnp.bfloat16),
            pltpu.SemaphoreType.DMA((2,)),
            pltpu.SemaphoreType.DMA((2,)),
            pltpu.SemaphoreType.DMA((2,)),
            pltpu.SemaphoreType.DMA((2,)),
            pltpu.SemaphoreType.DMA((2,)),
            pltpu.SemaphoreType.DMA((2,)),
        ]

    def bind(self, cells, main, edge, pack_out, pack_in, corner_out, corner_in, strip_in, *sems):
        self.cells, self.main, self.edge = cells, main, edge
        self.pack_out, self.pack_in = pack_out, pack_in
        self.corner_out, self.corner_in, self.strip_in = corner_out, corner_in, strip_in
        lon, lat = lax.axis_index("lon"), lax.axis_index("lat")
        lons, lats = self.sizes["lon"], self.sizes["lat"]
        self.south_open = lat > 0
        self.top = lat == lats - 1
        mirror = lons - 1 - lon
        self.left = {"lon": lax.rem(lon + lons - 1, lons)}
        self.right = {"lon": lax.rem(lon + 1, lons)}
        self.peers = [self.left, self.right, {"lon": mirror}]
        up = {
            "lon": jnp.where(self.top, mirror, lon),
            "lat": jnp.where(self.top, lat, lat + 1),
        }
        down = {"lat": jnp.where(self.south_open, lat - 1, lat + 1)}
        slot = jnp.where(self.top, 1, 0)
        lon_send, lon_recv, strip_send, strip_recv, corner_send, corner_recv = sems
        self.lon_copies = [
            self.copy(pack_out, pack_in.at[0], lon_send.at[0], lon_recv.at[0], self.left)
        ]
        if lons > 2:
            self.lon_copies.append(
                self.copy(pack_out, pack_in.at[1], lon_send.at[1], lon_recv.at[1], self.right)
            )
        high = cells.at[pl.ds(self.rows - self.margin, self.margin)]
        low = cells.at[pl.ds(0, self.margin)]
        self.up_strip = self.copy(high, strip_in.at[slot], strip_send.at[0], strip_recv.at[slot], up)
        self.down_strip = self.copy(low, strip_in.at[1], strip_send.at[1], strip_recv.at[1], down)
        self.up_corner = self.copy(
            corner_out, corner_in.at[slot], corner_send.at[0], corner_recv.at[slot], up
        )
        self.down_corner = self.copy(
            corner_out, corner_in.at[1], corner_send.at[1], corner_recv.at[1], down
        )
        self.arrivals = [
            [
                self.copy(low, strip_in.at[side], strip_send.at[0], strip_recv.at[side], up),
                self.copy(corner_out, corner_in.at[side], corner_send.at[0], corner_recv.at[side], up),
            ]
            for side in range(2)
        ]
        self.lane = lax.broadcasted_iota(jnp.int32, (self.channels, self.width), 1)

    def copy(self, src, dst, send_sem, recv_sem, device):
        return pltpu.make_async_remote_copy(
            src_ref=src,
            dst_ref=dst,
            send_sem=send_sem,
            recv_sem=recv_sem,
            device_id=device,
            device_id_type=pl.DeviceIdType.MESH,
        )

    def pack_columns(self):
        packed = jnp.zeros((self.channels, self.width), jnp.float32)
        for row in range(self.rows):
            turned = pltpu.roll(
                self.cells[row].astype(jnp.float32), row * self.pitch + self.margin, 1
            )
            packed = jnp.where(self.lane >= row * self.pitch, turned, packed)
        self.pack_out[...] = packed.astype(jnp.bfloat16)

    def unpacked(self, packed, row):
        shift = (self.width - row * self.pitch - self.margin) % self.width
        return pltpu.roll(packed, shift, 1)

    def start(self):
        for copy in self.lon_copies:
            copy.start()
        self.up_strip.start()
        pl.when(self.south_open)(self.down_strip.start)

    def spread_rows(self):
        for row in range(self.rows):
            self.main[self.margin + row] = self.cells[row].astype(jnp.float32)

    def forward_corners(self):
        for copy in self.lon_copies:
            copy.wait_recv()
        packed = self.pack_in[0].astype(jnp.float32)
        if len(self.lon_copies) > 1:
            from_left = self.pack_in[1].astype(jnp.float32)
            packed = jnp.where(lax.rem(self.lane, self.pitch) < self.margin, from_left, packed)
        self.corner_out[...] = packed.astype(jnp.bfloat16)
        self.up_corner.start()
        pl.when(self.south_open)(self.down_corner.start)
        for row in range(self.rows):
            self.edge[self.margin + row] = self.unpacked(packed, row)

    def finish(self):
        margin, rows = self.margin, self.rows

        @pl.when(self.south_open)
        def _():
            for copy in self.arrivals[0]:
                copy.wait_recv()
            packed = self.corner_in[0].astype(jnp.float32)
            for at in range(margin):
                self.main[at] = self.strip_in[0, at].astype(jnp.float32)
                self.edge[at] = self.unpacked(packed, rows - margin + at)

        @pl.when(jnp.logical_not(self.south_open))
        def _():
            for at in range(margin):
                self.main[at] = jnp.zeros((self.channels, self.width), jnp.float32)
                self.edge[at] = jnp.zeros((self.channels, self.width), jnp.float32)

        for copy in self.arrivals[1]:
            copy.wait_recv()
        north = margin + rows

        @pl.when(self.top)
        def _():
            one = lax.broadcasted_iota(jnp.int32, (self.width, self.width), 0)
            two = lax.broadcasted_iota(jnp.int32, (self.width, self.width), 1)
            turn = jnp.where(one + two == self.width - 1, 1.0, 0.0).astype(jnp.bfloat16)
            packed = self.corner_in[1].astype(jnp.float32)
            for at in range(margin):
                self.main[north + at] = jnp.dot(
                    self.strip_in[1, margin - 1 - at], turn, preferred_element_type=jnp.float32
                )
                sides = self.unpacked(packed, rows - 1 - at).astype(jnp.bfloat16)
                self.edge[north + at] = jnp.dot(sides, turn, preferred_element_type=jnp.float32)

        @pl.when(jnp.logical_not(self.top))
        def _():
            packed = self.corner_in[1].astype(jnp.float32)
            for at in range(margin):
                self.main[north + at] = self.strip_in[1, at].astype(jnp.float32)
                self.edge[north + at] = self.unpacked(packed, at)

    def drain(self):
        for copy in self.lon_copies + [self.up_strip, self.up_corner]:
            copy.wait_send()
        pl.when(self.south_open)(self.down_strip.wait_send)
        pl.when(self.south_open)(self.down_corner.wait_send)


def block_kernel(
    big,
    small,
    halo,
    scale,
    cells_ref,
    cot_ref,
    mask_ref,
    dw_ref,
    gain_ref,
    expand_ref,
    reduce_ref,
    state_out,
    expand_out,
    reduce_out,
    taps_out,
    gain_out,
    main_ref,
    edge_ref,
    expand_t,
    reduce_t,
    conv,
    scaled_all,
    hidden_all,
    d_pre_all,
    gain_sum,
    *scratch,
):
    channels, hidden_units = expand_ref.shape
    eights = channels // 8
    margin = KS // 2
    tile_rows = main_ref.shape[0] - 2 * margin
    width = main_ref.shape[2]
    spans = lane_spans(hidden_units)
    big.bind(*scratch[:8])
    small.bind(*scratch[8:16])
    halo.bind(cells_ref, main_ref, edge_ref, *scratch[16:])
    peers = big.peers() + small.peers() + halo.peers
    barrier_count = len(peers)
    barrier = pltpu.get_barrier_semaphore()
    for device in peers:
        pl.semaphore_signal(
            barrier, inc=1, device_id=device, device_id_type=pl.DeviceIdType.MESH
        )
    halo.pack_columns()
    pl.semaphore_wait(barrier, barrier_count)
    halo.start()
    big.clear()
    small.clear()
    gain_sum[...] = jnp.zeros_like(gain_sum)
    for low, high in spans:
        piece = expand_ref[:, low:high].astype(jnp.float32).T
        expand_t[low:high, :] = piece.astype(jnp.bfloat16)
        piece = reduce_ref[low:high, :].astype(jnp.float32).T
        reduce_t[:, low:high] = piece.astype(jnp.bfloat16)
    halo.spread_rows()
    halo.forward_corners()
    halo.finish()
    lane = lax.broadcasted_iota(jnp.int32, (8, width), 1)

    def conv_step(step, carry):
        rows = pl.ds(pl.multiple_of(step * 8, 8), 8)
        taps = dw_ref[rows, :]
        sums = [jnp.zeros((8, width), jnp.float32) for _ in range(tile_rows)]
        for shift_b in range(KS):
            weights = [
                jnp.broadcast_to(taps[:, a * KS + shift_b : a * KS + shift_b + 1], (8, width))
                for a in range(KS)
            ]
            for row in range(tile_rows + 2 * margin):
                cells = window(main_ref[row, rows, :], edge_ref[row, rows, :], lane, shift_b - margin)
                for shift_a in range(KS):
                    if 0 <= row - shift_a < tile_rows:
                        sums[row - shift_a] = sums[row - shift_a] + weights[shift_a] * cells
        for row in range(tile_rows):
            conv[rows, row * width : (row + 1) * width] = sums[row]
        return carry

    lax.fori_loop(0, eights, conv_step, 0)

    gain = gain_ref[...]
    block_rows = 2
    block = block_rows * width

    def cell_step(step, carry):
        cells = pl.ds(pl.multiple_of(step * block, block), block)
        conv_blk = conv[:, cells]
        centred = conv_blk - jnp.mean(conv_blk, axis=0, keepdims=True)
        inv_std = lax.rsqrt(jnp.mean(centred * centred, axis=0, keepdims=True) + norm_eps)
        normed = centred * inv_std
        scaled = (normed * gain).astype(jnp.bfloat16)
        scaled_all[:, cells] = scaled
        pre_act = jnp.dot(expand_t[...], scaled, preferred_element_type=jnp.float32)
        normal_cdf = 0.5 * (1.0 + lax.erf(pre_act * root_half))
        normal_pdf = jnp.exp(-0.5 * pre_act * pre_act) * gauss_norm
        hidden = (pre_act * normal_cdf).astype(jnp.bfloat16)
        gelu_slope = normal_cdf + pre_act * normal_pdf
        d_hidden = jnp.dot(reduce_ref[...], cot_ref[:, cells], preferred_element_type=jnp.float32)
        d_pre = (d_hidden * gelu_slope).astype(jnp.bfloat16)
        hidden_all[:, cells] = hidden
        d_pre_all[:, cells] = d_pre
        branch = jnp.dot(reduce_t[...], hidden, preferred_element_type=jnp.float32)
        for part in range(block_rows):
            row = step * block_rows + part
            at = pl.ds(pl.multiple_of(row * width, width), width)
            total = main_ref[margin + row] + branch[:, part * width : (part + 1) * width]
            state_out[:, at] = (total * mask_ref[:, at]).astype(jnp.bfloat16)
        d_scaled = jnp.dot(expand_ref[...], d_pre, preferred_element_type=jnp.float32)
        product = d_scaled * normed
        for part in range(block_rows):
            gain_sum[...] += product[:, part * width : (part + 1) * width]
        d_normed = d_scaled * gain
        mean_one = jnp.mean(d_normed, axis=0, keepdims=True)
        mean_two = jnp.mean(d_normed * normed, axis=0, keepdims=True)
        conv[:, cells] = inv_std * (d_normed - mean_one - normed * mean_two)
        return carry

    lax.fori_loop(0, tile_rows // block_rows, cell_step, 0)

    over_cells = (((1,), (1,)), ((), ()))
    for at, (low, high) in enumerate(spans):
        grad = lax.dot_general(
            scaled_all[...], d_pre_all[low:high, :], over_cells, preferred_element_type=jnp.float32
        )
        pack(big.acc, at * 2 * eights, 0, grad * scale)
        grad = lax.dot_general(
            cot_ref[...], hidden_all[low:high, :], over_cells, preferred_element_type=jnp.float32
        )
        pack(big.acc, at * 2 * eights, eights, grad * scale)

    def depthwise_step(step, carry):
        rows = pl.ds(pl.multiple_of(step * 8, 8), 8)
        d_conv = [conv[rows, row * width : (row + 1) * width] for row in range(tile_rows)]
        line = jnp.sum(gain_sum[rows, :], axis=1, keepdims=True)
        line = jnp.where(lane == KS * KS, line, 0.0)
        for shift_b in range(KS):
            sums = [jnp.zeros((8, width), jnp.float32) for _ in range(KS)]
            for row in range(tile_rows + 2 * margin):
                cells = window(main_ref[row, rows, :], edge_ref[row, rows, :], lane, shift_b - margin)
                for shift_a in range(KS):
                    if 0 <= row - shift_a < tile_rows:
                        sums[shift_a] = sums[shift_a] + d_conv[row - shift_a] * cells
            for shift_a in range(KS):
                total = jnp.sum(sums[shift_a], axis=1, keepdims=True)
                line = jnp.where(lane == shift_a * KS + shift_b, total, line)
        small.acc[pl.ds(step, 1)] = (line[:, :LANES] * scale).reshape(1, 8, LANES)
        return carry

    ahead, behind = big.steps(), small.steps()
    next(ahead)
    lax.fori_loop(0, eights // 2, depthwise_step, 0)
    next(ahead)
    lax.fori_loop(eights // 2, eights, depthwise_step, 0)
    running = [behind, ahead]
    while running:
        running = [one for one in running if next(one, None) is not None]

    for at, (low, high) in enumerate(spans):
        both = big.full[at * eights : (at + 1) * eights].astype(jnp.float32)
        both = both.reshape(2 * channels, LANES)
        expand_out[:, low:high] = both[:channels, : high - low]
        reduce_out[low:high, :] = both[channels:].T[: high - low, :]
    rest = small.full[: -(-eights // 2)].astype(jnp.float32).reshape(-1, LANES)
    taps_out[...] = rest[:channels, : KS * KS]
    gain_out[...] = rest[:channels, KS * KS : KS * KS + 1]
    halo.drain()


def block_call(sizes, scale, masked, cot, mask, dw_weight, norm_gain, expand_weight, reduce_weight):
    channels, hidden = expand_weight.shape
    cells = cot.shape[1]
    eights = channels // 8
    big = Reducer(sizes, big_streams(sizes), -(-hidden // LANES) * eights)
    small = Reducer(sizes, small_streams(sizes), -(-eights // 2))
    rows, _, width = masked.shape
    halo = Halo(sizes, KS // 2, rows, channels, width)
    padded = pltpu.VMEM((rows + 2 * (KS // 2), channels, width), jnp.float32)
    vmem = pl.BlockSpec(memory_space=pltpu.VMEM)
    return pl.pallas_call(
        functools.partial(block_kernel, big, small, halo, scale),
        out_shape=(
            jax.ShapeDtypeStruct((channels, cells), jnp.bfloat16),
            jax.ShapeDtypeStruct((channels, hidden), jnp.float32),
            jax.ShapeDtypeStruct((hidden, channels), jnp.float32),
            jax.ShapeDtypeStruct((channels, KS * KS), jnp.float32),
            jax.ShapeDtypeStruct((channels, 1), jnp.float32),
        ),
        in_specs=[vmem] * 7,
        out_specs=[vmem] * 5,
        scratch_shapes=[
            padded,
            padded,
            pltpu.VMEM((hidden, channels), jnp.bfloat16),
            pltpu.VMEM((channels, hidden), jnp.bfloat16),
            pltpu.VMEM((channels, cells), jnp.float32),
            pltpu.VMEM((channels, cells), jnp.bfloat16),
            pltpu.VMEM((hidden, cells), jnp.bfloat16),
            pltpu.VMEM((hidden, cells), jnp.bfloat16),
            pltpu.VMEM((channels, width), jnp.float32),
        ]
        + big.scratch()
        + small.scratch()
        + halo.scratch(),
        compiler_params=pltpu.CompilerParams(
            collective_id=0, has_side_effects=True, vmem_limit_bytes=60 * 1024 * 1024
        ),
    )(masked, cot, mask, dw_weight, norm_gain[:, None], expand_weight, reduce_weight)


def body(ocean_state, ocean_mask, dw_weight, norm_gain, expand_weight, reduce_weight, cotangent):
    state_tile = ocean_state[0]
    channels, tile_rows, tile_cols = state_tile.shape
    mask_bf = ocean_mask.astype(jnp.bfloat16)
    masked = (state_tile * mask_bf[None]).transpose(1, 0, 2)
    cell_count = tile_rows * tile_cols
    cot_masked = (cotangent[0] * mask_bf[None]).reshape(channels, cell_count)
    sizes = {axis: lax.axis_size(axis) for axis in MESH_AXES}
    grad_scale = 1.0 / math.sqrt(math.prod(sizes.values()) * cell_count)
    out_flat, grad_expand, grad_reduce, taps, gain = block_call(
        sizes,
        grad_scale,
        masked,
        cot_masked,
        ocean_mask.astype(jnp.float32).reshape(1, cell_count),
        dw_weight,
        norm_gain,
        expand_weight,
        reduce_weight,
    )
    next_state = out_flat.reshape(channels, tile_rows, tile_cols)[None]
    return (next_state, taps, gain[:, 0], grad_expand, grad_reduce)


def solution(mesh):
    return jax.shard_map(
        body,
        mesh=mesh,
        in_specs=(
            P("ens", None, "lat", "lon"),
            P("lat", "lon"),
            P(),
            P(),
            P(),
            P(),
            P("ens", None, "lat", "lon"),
        ),
        out_specs=(P("ens", None, "lat", "lon"), P(), P(), P(), P()),
        check_vma=False,
    )
```

```python
import functools
import math

import jax
import jax.numpy as jnp
from jax import lax
from jax.experimental import pallas as pl
from jax.experimental.pallas import tpu as pltpu
from jax.sharding import PartitionSpec as P

KS = 7


norm_eps = 1e-06
root_half = 0.7071067811865476
gauss_norm = 0.3989422804014327


MESH_AXES = ("ens", "lon", "lat")
TILE = 16
LANES = 128


def bits_of(axis, size, first=0):
    return [(axis, 1 << k, 2) for k in range(first, size.bit_length() - 1)]


def big_streams(sizes):
    lead = bits_of("lat", sizes["lat"])[:1]
    groups = [bits_of("lat", sizes["lat"], 1), bits_of("lon", sizes["lon"])]
    groups.append([("ens", 1, sizes["ens"])])
    groups = [[digit for digit in group if digit[2] > 1] for group in groups]
    streams = []
    for turn in range(3):
        order = groups[turn:] + groups[:turn]
        streams.append(lead + [digit for group in order for digit in group])
    return streams


def small_streams(sizes):
    stages = []
    for axis in ("lat", "lon", "ens"):
        whole = [(axis, 1, sizes[axis])] if sizes[axis] <= 4 else bits_of(axis, sizes[axis])
        stages += [digit for digit in whole if digit[2] > 1]
    return [stages]


class Reducer:
    def __init__(self, sizes, streams, tiles_used):
        self.streams = streams
        self.count = math.prod(sizes.values())
        share = -(-tiles_used // len(self.streams))
        self.share = -(-share // self.count) * self.count
        self.tiles = self.share * len(self.streams)
        slots = []
        for number, stages in enumerate(self.streams):
            extent = self.share
            place = number * self.share
            for level, (axis, stride, radix) in enumerate(stages):
                extent //= radix
                for turn in range(1, radix):
                    slots.append((number, level, turn, place))
                    place += extent
        self.slots = {(n, v, t): (i, p) for i, (n, v, t, p) in enumerate(slots)}

    def scratch(self):
        n = len(self.slots)
        return [
            pltpu.VMEM((2 * self.tiles, 8, LANES), jnp.float32),
            pltpu.VMEM((self.tiles, TILE, LANES), jnp.bfloat16),
            pltpu.VMEM((self.tiles, TILE, LANES), jnp.bfloat16),
            pltpu.VMEM((self.tiles, TILE, LANES), jnp.bfloat16),
            pltpu.SemaphoreType.DMA((n,)),
            pltpu.SemaphoreType.DMA((n,)),
            pltpu.SemaphoreType.DMA((n,)),
            pltpu.SemaphoreType.DMA((n,)),
        ]

    def bind(self, acc, send, recv, full, ss, rs, sg, rg):
        self.acc, self.send, self.recv, self.full = acc, send, recv, full
        self.ss, self.rs, self.sg, self.rg = ss, rs, sg, rg
        where = {axis: lax.axis_index(axis) for axis in MESH_AXES}
        self.where = where
        self.starts = []
        self.extents = []
        for number, stages in enumerate(self.streams):
            start = number * self.share
            extent = self.share
            starts, extents = [start], [extent]
            for axis, stride, radix in stages:
                extent //= radix
                start = start + lax.rem(lax.div(where[axis], stride), radix) * extent
                starts.append(start)
                extents.append(extent)
            self.starts.append(starts)
            self.extents.append(extents)
        return self

    def peer(self, digit, turn):
        axis, stride, radix = digit
        mine = lax.rem(lax.div(self.where[axis], stride), radix)
        theirs = lax.rem(mine + turn, radix)
        return theirs, {axis: self.where[axis] + (theirs - mine) * stride}

    def peers(self):
        seen = set()
        found = []
        for stages in self.streams:
            for digit in stages:
                for turn in range(1, digit[2]):
                    if (digit, turn) not in seen:
                        seen.add((digit, turn))
                        found.append(self.peer(digit, turn)[1])
        return found

    def scatter_copy(self, number, level, turn):
        digit = self.streams[number][level]
        extent = self.extents[number][level + 1]
        theirs, device = self.peer(digit, turn)
        begin = self.starts[number][level] + theirs * extent
        slot, place = self.slots[number, level, turn]
        copy = pltpu.make_async_remote_copy(
            src_ref=self.send.at[pl.ds(begin, extent)],
            dst_ref=self.recv.at[pl.ds(place, extent)],
            send_sem=self.ss.at[slot],
            recv_sem=self.rs.at[slot],
            device_id=device,
            device_id_type=pl.DeviceIdType.MESH,
        )
        return copy, begin, extent, place

    def scatter_start(self, number, level):
        for turn in range(1, self.streams[number][level][2]):
            copy, begin, extent, _ = self.scatter_copy(number, level, turn)
            piece = self.acc[pl.ds(2 * begin, 2 * extent)].astype(jnp.bfloat16)
            self.send[pl.ds(begin, extent)] = piece.reshape(extent, TILE, LANES)
            copy.start()

    def scatter_finish(self, number, level):
        begin = self.starts[number][level + 1]
        extent = self.extents[number][level + 1]
        total = self.acc[pl.ds(2 * begin, 2 * extent)]
        for turn in range(1, self.streams[number][level][2]):
            copy, _, _, place = self.scatter_copy(number, level, turn)
            copy.wait_recv()
            piece = self.recv[pl.ds(place, extent)].astype(jnp.float32)
            total = total + piece.reshape(2 * extent, 8, LANES)
        self.acc[pl.ds(2 * begin, 2 * extent)] = total

    def gather_copy(self, number, level, turn):
        _, device = self.peer(self.streams[number][level], turn)
        begin = self.starts[number][level + 1]
        extent = self.extents[number][level + 1]
        slot, _ = self.slots[number, level, turn]
        block = self.full.at[pl.ds(begin, extent)]
        return pltpu.make_async_remote_copy(
            src_ref=block,
            dst_ref=block,
            send_sem=self.sg.at[slot],
            recv_sem=self.rg.at[slot],
            device_id=device,
            device_id_type=pl.DeviceIdType.MESH,
        )

    def turns(self, number, level):
        return range(1, self.streams[number][level][2])

    def gather_start(self, number, level):
        for turn in self.turns(number, level):
            self.gather_copy(number, level, turn).start()

    def gather_finish(self, number, level):
        for turn in self.turns(number, level):
            self.gather_copy(number, level, turn).wait_recv()

    def clear(self):
        self.acc[...] = jnp.zeros_like(self.acc)

    def steps(self):
        numbers = range(len(self.streams))
        depth = len(self.streams[0])
        for number in numbers:
            self.scatter_start(number, 0)
        yield True
        for level in range(depth):
            for number in numbers:
                self.scatter_finish(number, level)
                if level + 1 < depth:
                    self.scatter_start(number, level + 1)
                else:
                    begin, extent = self.starts[number][-1], self.extents[number][-1]
                    mine = self.acc[pl.ds(2 * begin, 2 * extent)].astype(jnp.bfloat16)
                    self.full[pl.ds(begin, extent)] = mine.reshape(extent, TILE, LANES)
                    self.gather_start(number, level)
            yield True
        for level in reversed(range(depth)):
            for number in numbers:
                self.gather_finish(number, level)
                if level > 0:
                    self.gather_start(number, level - 1)
            yield True
        for number in numbers:
            for level in range(depth):
                for turn in self.turns(number, level):
                    self.scatter_copy(number, level, turn)[0].wait_send()
                    self.gather_copy(number, level, turn).wait_send()


def pack(acc, lane_tile, row_tile, block):
    rows, width = block.shape
    begin = lane_tile + row_tile
    acc[begin : begin + rows // 8, :, :width] = block.reshape(rows // 8, 8, width)


def lane_spans(width):
    return [(low, min(low + LANES, width)) for low in range(0, width, LANES)]


def window(main, edge, lane, shift):
    width = main.shape[1]
    if shift == 0:
        return main
    outside = lane < shift if shift > 0 else lane >= width + shift
    return pltpu.roll(jnp.where(outside, edge, main), (-shift) % width, 1)


class Halo:
    def __init__(self, sizes, margin, rows, channels, width):
        self.sizes, self.margin, self.rows = sizes, margin, rows
        self.channels, self.width = channels, width
        self.pitch = width // rows

    def scratch(self):
        packed = (self.channels, self.width)
        return [
            pltpu.VMEM(packed, jnp.bfloat16),
            pltpu.VMEM((2,) + packed, jnp.bfloat16),
            pltpu.VMEM(packed, jnp.bfloat16),
            pltpu.VMEM((2,) + packed, jnp.bfloat16),
            pltpu.VMEM((2, self.margin) + packed, jnp.bfloat16),
            pltpu.SemaphoreType.DMA((2,)),
            pltpu.SemaphoreType.DMA((2,)),
            pltpu.SemaphoreType.DMA((2,)),
            pltpu.SemaphoreType.DMA((2,)),
            pltpu.SemaphoreType.DMA((2,)),
            pltpu.SemaphoreType.DMA((2,)),
        ]

    def bind(self, cells, main, edge, pack_out, pack_in, corner_out, corner_in, strip_in, *sems):
        self.cells, self.main, self.edge = cells, main, edge
        self.pack_out, self.pack_in = pack_out, pack_in
        self.corner_out, self.corner_in, self.strip_in = corner_out, corner_in, strip_in
        lon, lat = lax.axis_index("lon"), lax.axis_index("lat")
        lons, lats = self.sizes["lon"], self.sizes["lat"]
        self.south_open = lat > 0
        self.top = lat == lats - 1
        mirror = lons - 1 - lon
        self.left = {"lon": lax.rem(lon + lons - 1, lons)}
        self.right = {"lon": lax.rem(lon + 1, lons)}
        self.peers = [self.left, self.right, {"lon": mirror}]
        up = {
            "lon": jnp.where(self.top, mirror, lon),
            "lat": jnp.where(self.top, lat, lat + 1),
        }
        down = {"lat": jnp.where(self.south_open, lat - 1, lat + 1)}
        slot = jnp.where(self.top, 1, 0)
        lon_send, lon_recv, strip_send, strip_recv, corner_send, corner_recv = sems
        self.lon_copies = [
            self.copy(pack_out, pack_in.at[0], lon_send.at[0], lon_recv.at[0], self.left)
        ]
        if lons > 2:
            self.lon_copies.append(
                self.copy(pack_out, pack_in.at[1], lon_send.at[1], lon_recv.at[1], self.right)
            )
        high = cells.at[pl.ds(self.rows - self.margin, self.margin)]
        low = cells.at[pl.ds(0, self.margin)]
        self.up_strip = self.copy(high, strip_in.at[slot], strip_send.at[0], strip_recv.at[slot], up)
        self.down_strip = self.copy(low, strip_in.at[1], strip_send.at[1], strip_recv.at[1], down)
        self.up_corner = self.copy(
            corner_out, corner_in.at[slot], corner_send.at[0], corner_recv.at[slot], up
        )
        self.down_corner = self.copy(
            corner_out, corner_in.at[1], corner_send.at[1], corner_recv.at[1], down
        )
        self.arrivals = [
            [
                self.copy(low, strip_in.at[side], strip_send.at[0], strip_recv.at[side], up),
                self.copy(corner_out, corner_in.at[side], corner_send.at[0], corner_recv.at[side], up),
            ]
            for side in range(2)
        ]
        self.lane = lax.broadcasted_iota(jnp.int32, (self.channels, self.width), 1)

    def copy(self, src, dst, send_sem, recv_sem, device):
        return pltpu.make_async_remote_copy(
            src_ref=src,
            dst_ref=dst,
            send_sem=send_sem,
            recv_sem=recv_sem,
            device_id=device,
            device_id_type=pl.DeviceIdType.MESH,
        )

    def pack_columns(self):
        packed = jnp.zeros((self.channels, self.width), jnp.float32)
        for row in range(self.rows):
            turned = pltpu.roll(
                self.cells[row].astype(jnp.float32), row * self.pitch + self.margin, 1
            )
            packed = jnp.where(self.lane >= row * self.pitch, turned, packed)
        self.pack_out[...] = packed.astype(jnp.bfloat16)

    def unpacked(self, packed, row):
        shift = (self.width - row * self.pitch - self.margin) % self.width
        return pltpu.roll(packed, shift, 1)

    def start(self):
        for copy in self.lon_copies:
            copy.start()
        self.up_strip.start()
        pl.when(self.south_open)(self.down_strip.start)

    def spread_rows(self):
        for row in range(self.rows):
            self.main[self.margin + row] = self.cells[row].astype(jnp.float32)

    def forward_corners(self):
        for copy in self.lon_copies:
            copy.wait_recv()
        packed = self.pack_in[0].astype(jnp.float32)
        if len(self.lon_copies) > 1:
            from_left = self.pack_in[1].astype(jnp.float32)
            packed = jnp.where(lax.rem(self.lane, self.pitch) < self.margin, from_left, packed)
        self.corner_out[...] = packed.astype(jnp.bfloat16)
        self.up_corner.start()
        pl.when(self.south_open)(self.down_corner.start)
        for row in range(self.rows):
            self.edge[self.margin + row] = self.unpacked(packed, row)

    def finish(self):
        margin, rows = self.margin, self.rows

        @pl.when(self.south_open)
        def _():
            for copy in self.arrivals[0]:
                copy.wait_recv()
            packed = self.corner_in[0].astype(jnp.float32)
            for at in range(margin):
                self.main[at] = self.strip_in[0, at].astype(jnp.float32)
                self.edge[at] = self.unpacked(packed, rows - margin + at)

        @pl.when(jnp.logical_not(self.south_open))
        def _():
            for at in range(margin):
                self.main[at] = jnp.zeros((self.channels, self.width), jnp.float32)
                self.edge[at] = jnp.zeros((self.channels, self.width), jnp.float32)

        for copy in self.arrivals[1]:
            copy.wait_recv()
        north = margin + rows

        @pl.when(self.top)
        def _():
            one = lax.broadcasted_iota(jnp.int32, (self.width, self.width), 0)
            two = lax.broadcasted_iota(jnp.int32, (self.width, self.width), 1)
            turn = jnp.where(one + two == self.width - 1, 1.0, 0.0).astype(jnp.bfloat16)
            packed = self.corner_in[1].astype(jnp.float32)
            for at in range(margin):
                self.main[north + at] = jnp.dot(
                    self.strip_in[1, margin - 1 - at], turn, preferred_element_type=jnp.float32
                )
                sides = self.unpacked(packed, rows - 1 - at).astype(jnp.bfloat16)
                self.edge[north + at] = jnp.dot(sides, turn, preferred_element_type=jnp.float32)

        @pl.when(jnp.logical_not(self.top))
        def _():
            packed = self.corner_in[1].astype(jnp.float32)
            for at in range(margin):
                self.main[north + at] = self.strip_in[1, at].astype(jnp.float32)
                self.edge[north + at] = self.unpacked(packed, at)

    def drain(self):
        for copy in self.lon_copies + [self.up_strip, self.up_corner]:
            copy.wait_send()
        pl.when(self.south_open)(self.down_strip.wait_send)
        pl.when(self.south_open)(self.down_corner.wait_send)


def block_kernel(
    big,
    small,
    halo,
    scale,
    cells_ref,
    cot_ref,
    mask_ref,
    dw_ref,
    gain_ref,
    expand_ref,
    reduce_t,
    state_out,
    expand_out,
    reduce_out,
    taps_out,
    gain_out,
    main_ref,
    edge_ref,
    expand_t,
    reduce_ref,
    table,
    table_t,
    conv,
    scaled_all,
    hidden_all,
    d_pre_all,
    gain_sum,
    *scratch,
):
    channels, hidden_units = expand_ref.shape
    eights = channels // 8
    margin = KS // 2
    tile_rows = main_ref.shape[0] - 2 * margin
    width = main_ref.shape[2]
    spans = lane_spans(hidden_units)
    big.bind(*scratch[:8])
    small.bind(*scratch[8:16])
    halo.bind(cells_ref, main_ref, edge_ref, *scratch[16:])
    peers = big.peers() + small.peers() + halo.peers
    barrier_count = len(peers)
    barrier = pltpu.get_barrier_semaphore()
    for device in peers:
        pl.semaphore_signal(
            barrier, inc=1, device_id=device, device_id_type=pl.DeviceIdType.MESH
        )
    halo.pack_columns()
    pl.semaphore_wait(barrier, barrier_count)
    halo.start()
    big.clear()
    small.clear()
    gain_sum[...] = jnp.zeros_like(gain_sum)
    for low, high in spans:
        piece = expand_ref[:, low:high].astype(jnp.float32).T
        expand_t[low:high, :] = piece.astype(jnp.bfloat16)
        piece = reduce_t[:, low:high].astype(jnp.float32).T
        reduce_ref[low:high, :] = piece.astype(jnp.bfloat16)
    table[...] = jnp.zeros_like(table)
    table[: KS * KS, :channels] = dw_ref[...]
    table[KS * KS : KS * KS + 1, :channels] = gain_ref[...]
    columns = table[...].T
    table_t[...] = columns
    gain = columns[:channels, KS * KS : KS * KS + 1]
    halo.spread_rows()
    halo.forward_corners()
    lane = lax.broadcasted_iota(jnp.int32, (8, width), 1)

    def conv_step(part, first, step, carry):
        rows = pl.ds(pl.multiple_of(step * 8, 8), 8)
        taps = table_t[rows, :]
        spans_of = [slice(row * width, (row + 1) * width) for row in range(tile_rows)]
        if first:
            sums = [jnp.zeros((8, width), jnp.float32) for _ in range(tile_rows)]
        else:
            sums = [conv[rows, one] for one in spans_of]
        for shift_b in range(KS):
            weights = [
                jnp.broadcast_to(taps[:, a * KS + shift_b : a * KS + shift_b + 1], (8, width))
                for a in range(KS)
            ]
            for row in part:
                cells = window(main_ref[row, rows, :], edge_ref[row, rows, :], lane, shift_b - margin)
                for shift_a in range(KS):
                    if 0 <= row - shift_a < tile_rows:
                        sums[row - shift_a] = sums[row - shift_a] + weights[shift_a] * cells
        for row in range(tile_rows):
            conv[rows, spans_of[row]] = sums[row]
        return carry

    inner = range(margin, margin + tile_rows)
    outer = [row for row in range(tile_rows + 2 * margin) if row not in inner]
    lax.fori_loop(0, eights, functools.partial(conv_step, inner, True), 0)
    halo.finish()
    lax.fori_loop(0, eights, functools.partial(conv_step, outer, False), 0)

    block_rows = 2
    block = block_rows * width

    def cell_step(step, carry):
        cells = pl.ds(pl.multiple_of(step * block, block), block)
        conv_blk = conv[:, cells]
        centred = conv_blk - jnp.mean(conv_blk, axis=0, keepdims=True)
        inv_std = lax.rsqrt(jnp.mean(centred * centred, axis=0, keepdims=True) + norm_eps)
        normed = centred * inv_std
        scaled = (normed * gain).astype(jnp.bfloat16)
        scaled_all[:, cells] = scaled
        pre_act = jnp.dot(expand_t[...], scaled, preferred_element_type=jnp.float32)
        normal_cdf = 0.5 * (1.0 + lax.erf(pre_act * root_half))
        normal_pdf = jnp.exp(-0.5 * pre_act * pre_act) * gauss_norm
        hidden = (pre_act * normal_cdf).astype(jnp.bfloat16)
        gelu_slope = normal_cdf + pre_act * normal_pdf
        d_hidden = jnp.dot(reduce_ref[...], cot_ref[:, cells], preferred_element_type=jnp.float32)
        d_pre = (d_hidden * gelu_slope).astype(jnp.bfloat16)
        hidden_all[:, cells] = hidden
        d_pre_all[:, cells] = d_pre
        branch = jnp.dot(reduce_t[...], hidden, preferred_element_type=jnp.float32)
        for part in range(block_rows):
            row = step * block_rows + part
            at = pl.ds(pl.multiple_of(row * width, width), width)
            total = main_ref[margin + row] + branch[:, part * width : (part + 1) * width]
            state_out[:, at] = (total * mask_ref[:, at]).astype(jnp.bfloat16)
        d_scaled = jnp.dot(expand_ref[...], d_pre, preferred_element_type=jnp.float32)
        product = d_scaled * normed
        for part in range(block_rows):
            gain_sum[...] += product[:, part * width : (part + 1) * width]
        d_normed = d_scaled * gain
        mean_one = jnp.mean(d_normed, axis=0, keepdims=True)
        mean_two = jnp.mean(d_normed * normed, axis=0, keepdims=True)
        conv[:, cells] = inv_std * (d_normed - mean_one - normed * mean_two)
        return carry

    lax.fori_loop(0, tile_rows // block_rows, cell_step, 0)

    over_cells = (((1,), (1,)), ((), ()))
    for low in range(0, hidden_units, 2 * LANES):
        high = min(low + 2 * LANES, hidden_units)
        for turn, (left, right) in enumerate([(scaled_all, d_pre_all), (cot_ref, hidden_all)]):
            grad = lax.dot_general(
                left[...], right[low:high, :], over_cells, preferred_element_type=jnp.float32
            )
            for first, last in lane_spans(high - low):
                at = (low + first) // LANES
                pack(big.acc, at * 2 * eights, turn * eights, grad[:, first:last] * scale)

    def depthwise_step(step, carry):
        rows = pl.ds(pl.multiple_of(step * 8, 8), 8)
        d_conv = [conv[rows, row * width : (row + 1) * width] for row in range(tile_rows)]
        line = jnp.sum(gain_sum[rows, :], axis=1, keepdims=True)
        line = jnp.where(lane == KS * KS, line, 0.0)
        for shift_b in range(KS):
            sums = [jnp.zeros((8, width), jnp.float32) for _ in range(KS)]
            for row in range(tile_rows + 2 * margin):
                cells = window(main_ref[row, rows, :], edge_ref[row, rows, :], lane, shift_b - margin)
                for shift_a in range(KS):
                    if 0 <= row - shift_a < tile_rows:
                        sums[shift_a] = sums[shift_a] + d_conv[row - shift_a] * cells
            for shift_a in range(KS):
                total = jnp.sum(sums[shift_a], axis=1, keepdims=True)
                line = jnp.where(lane == shift_a * KS + shift_b, total, line)
        small.acc[pl.ds(step, 1)] = (line[:, :LANES] * scale).reshape(1, 8, LANES)
        return carry

    ahead, behind = big.steps(), small.steps()
    next(ahead)
    lax.fori_loop(0, eights // 2, depthwise_step, 0)
    next(ahead)
    lax.fori_loop(eights // 2, eights, depthwise_step, 0)
    running = [behind, ahead]
    while running:
        running = [one for one in running if next(one, None) is not None]

    for at, (low, high) in enumerate(spans):
        both = big.full[at * eights : (at + 1) * eights].astype(jnp.float32)
        both = both.reshape(2 * channels, LANES)
        expand_out[:, low:high] = both[:channels, : high - low]
        reduce_out[:, low:high] = both[channels:, : high - low]
    table_t[:channels] = (
        small.full[: -(-eights // 2)].astype(jnp.float32).reshape(-1, LANES)[:channels]
    )
    lines = table_t[...].T
    taps_out[...] = lines[: KS * KS, :channels]
    gain_out[...] = lines[KS * KS : KS * KS + 1, :channels]
    halo.drain()


def block_call(sizes, scale, masked, cot, mask, dw_weight, norm_gain, expand_weight, reduce_weight):
    channels, hidden = expand_weight.shape
    cells = cot.shape[1]
    eights = channels // 8
    big = Reducer(sizes, big_streams(sizes), -(-hidden // LANES) * eights)
    small = Reducer(sizes, small_streams(sizes), -(-eights // 2))
    rows, _, width = masked.shape
    halo = Halo(sizes, KS // 2, rows, channels, width)
    padded = pltpu.VMEM((rows + 2 * (KS // 2), channels, width), jnp.float32)
    vmem = pl.BlockSpec(memory_space=pltpu.VMEM)
    return pl.pallas_call(
        functools.partial(block_kernel, big, small, halo, scale),
        out_shape=(
            jax.ShapeDtypeStruct((channels, cells), jnp.bfloat16),
            jax.ShapeDtypeStruct((channels, hidden), jnp.float32),
            jax.ShapeDtypeStruct((channels, hidden), jnp.float32),
            jax.ShapeDtypeStruct((KS * KS, channels), jnp.float32),
            jax.ShapeDtypeStruct((1, channels), jnp.float32),
        ),
        in_specs=[vmem] * 7,
        out_specs=[vmem] * 5,
        scratch_shapes=[
            padded,
            padded,
            pltpu.VMEM((hidden, channels), jnp.bfloat16),
            pltpu.VMEM((hidden, channels), jnp.bfloat16),
            pltpu.VMEM((LANES, -(-channels // LANES) * LANES), jnp.float32),
            pltpu.VMEM((-(-channels // LANES) * LANES, LANES), jnp.float32),
            pltpu.VMEM((channels, cells), jnp.float32),
            pltpu.VMEM((channels, cells), jnp.bfloat16),
            pltpu.VMEM((hidden, cells), jnp.bfloat16),
            pltpu.VMEM((hidden, cells), jnp.bfloat16),
            pltpu.VMEM((channels, width), jnp.float32),
        ]
        + big.scratch()
        + small.scratch()
        + halo.scratch(),
        compiler_params=pltpu.CompilerParams(
            collective_id=0, has_side_effects=True, vmem_limit_bytes=60 * 1024 * 1024
        ),
    )(masked, cot, mask, dw_weight.T, norm_gain[None, :], expand_weight, reduce_weight.T)


def body(ocean_state, ocean_mask, dw_weight, norm_gain, expand_weight, reduce_weight, cotangent):
    state_tile = ocean_state[0]
    channels, tile_rows, tile_cols = state_tile.shape
    mask_bf = ocean_mask.astype(jnp.bfloat16)
    masked = (state_tile * mask_bf[None]).transpose(1, 0, 2)
    cell_count = tile_rows * tile_cols
    cot_masked = (cotangent[0] * mask_bf[None]).reshape(channels, cell_count)
    sizes = {axis: lax.axis_size(axis) for axis in MESH_AXES}
    grad_scale = 1.0 / math.sqrt(math.prod(sizes.values()) * cell_count)
    out_flat, grad_expand, grad_reduce, taps, gain = block_call(
        sizes,
        grad_scale,
        masked,
        cot_masked,
        ocean_mask.astype(jnp.float32).reshape(1, cell_count),
        dw_weight,
        norm_gain,
        expand_weight,
        reduce_weight,
    )
    next_state = out_flat.reshape(channels, tile_rows, tile_cols)[None]
    return (next_state, taps.T, gain[0], grad_expand, grad_reduce.T)


def solution(mesh):
    return jax.shard_map(
        body,
        mesh=mesh,
        in_specs=(
            P("ens", None, "lat", "lon"),
            P("lat", "lon"),
            P(),
            P(),
            P(),
            P(),
            P("ens", None, "lat", "lon"),
        ),
        out_specs=(P("ens", None, "lat", "lon"), P(), P(), P(), P()),
        check_vma=False,
    )
```

```python
import functools
import math

import jax
import jax.numpy as jnp
from jax import lax
from jax.experimental import pallas as pl
from jax.experimental.pallas import tpu as pltpu
from jax.sharding import PartitionSpec as P

KS = 7


norm_eps = 1e-06
root_half = 0.7071067811865476
gauss_norm = 0.3989422804014327


MESH_AXES = ("ens", "lon", "lat")
TILE = 16
LANES = 128


def bits_of(axis, size, first=0):
    return [(axis, 1 << k, 2) for k in range(first, size.bit_length() - 1)]


def big_streams(sizes):
    lead = bits_of("lat", sizes["lat"])[:1]
    groups = [bits_of("lat", sizes["lat"], 1), bits_of("lon", sizes["lon"])]
    groups.append([("ens", 1, sizes["ens"])])
    groups = [[digit for digit in group if digit[2] > 1] for group in groups]
    streams = []
    for turn in range(3):
        order = groups[turn:] + groups[:turn]
        streams.append(lead + [digit for group in order for digit in group])
    return streams


def small_streams(sizes):
    stages = []
    for axis in ("lat", "lon", "ens"):
        whole = [(axis, 1, sizes[axis])] if sizes[axis] <= 4 else bits_of(axis, sizes[axis])
        stages += [digit for digit in whole if digit[2] > 1]
    return [stages]


class Reducer:
    def __init__(self, sizes, streams, tiles_used):
        self.streams = streams
        self.count = math.prod(sizes.values())
        share = -(-tiles_used // len(self.streams))
        self.share = -(-share // self.count) * self.count
        self.tiles = self.share * len(self.streams)
        slots = []
        for number, stages in enumerate(self.streams):
            extent = self.share
            place = number * self.share
            for level, (axis, stride, radix) in enumerate(stages):
                extent //= radix
                for turn in range(1, radix):
                    slots.append((number, level, turn, place))
                    place += extent
        self.slots = {(n, v, t): (i, p) for i, (n, v, t, p) in enumerate(slots)}

    def scratch(self):
        n = len(self.slots)
        return [
            pltpu.VMEM((2 * self.tiles, 8, LANES), jnp.float32),
            pltpu.VMEM((self.tiles, TILE, LANES), jnp.bfloat16),
            pltpu.VMEM((self.tiles, TILE, LANES), jnp.bfloat16),
            pltpu.VMEM((self.tiles, TILE, LANES), jnp.bfloat16),
            pltpu.SemaphoreType.DMA((n,)),
            pltpu.SemaphoreType.DMA((n,)),
            pltpu.SemaphoreType.DMA((n,)),
            pltpu.SemaphoreType.DMA((n,)),
        ]

    def bind(self, acc, send, recv, full, ss, rs, sg, rg):
        self.acc, self.send, self.recv, self.full = acc, send, recv, full
        self.ss, self.rs, self.sg, self.rg = ss, rs, sg, rg
        where = {axis: lax.axis_index(axis) for axis in MESH_AXES}
        self.where = where
        self.starts = []
        self.extents = []
        for number, stages in enumerate(self.streams):
            start = number * self.share
            extent = self.share
            starts, extents = [start], [extent]
            for axis, stride, radix in stages:
                extent //= radix
                start = start + lax.rem(lax.div(where[axis], stride), radix) * extent
                starts.append(start)
                extents.append(extent)
            self.starts.append(starts)
            self.extents.append(extents)
        return self

    def peer(self, digit, turn):
        axis, stride, radix = digit
        mine = lax.rem(lax.div(self.where[axis], stride), radix)
        theirs = lax.rem(mine + turn, radix)
        return theirs, {axis: self.where[axis] + (theirs - mine) * stride}

    def peers(self):
        seen = set()
        found = []
        for stages in self.streams:
            for digit in stages:
                for turn in range(1, digit[2]):
                    if (digit, turn) not in seen:
                        seen.add((digit, turn))
                        found.append(self.peer(digit, turn)[1])
        return found

    def scatter_copy(self, number, level, turn):
        digit = self.streams[number][level]
        extent = self.extents[number][level + 1]
        theirs, device = self.peer(digit, turn)
        begin = self.starts[number][level] + theirs * extent
        slot, place = self.slots[number, level, turn]
        copy = pltpu.make_async_remote_copy(
            src_ref=self.send.at[pl.ds(begin, extent)],
            dst_ref=self.recv.at[pl.ds(place, extent)],
            send_sem=self.ss.at[slot],
            recv_sem=self.rs.at[slot],
            device_id=device,
            device_id_type=pl.DeviceIdType.MESH,
        )
        return copy, begin, extent, place

    def scatter_start(self, number, level):
        for turn in range(1, self.streams[number][level][2]):
            copy, begin, extent, _ = self.scatter_copy(number, level, turn)
            piece = self.acc[pl.ds(2 * begin, 2 * extent)].astype(jnp.bfloat16)
            self.send[pl.ds(begin, extent)] = piece.reshape(extent, TILE, LANES)
            copy.start()

    def scatter_finish(self, number, level):
        begin = self.starts[number][level + 1]
        extent = self.extents[number][level + 1]
        total = self.acc[pl.ds(2 * begin, 2 * extent)]
        for turn in range(1, self.streams[number][level][2]):
            copy, _, _, place = self.scatter_copy(number, level, turn)
            copy.wait_recv()
            piece = self.recv[pl.ds(place, extent)].astype(jnp.float32)
            total = total + piece.reshape(2 * extent, 8, LANES)
        self.acc[pl.ds(2 * begin, 2 * extent)] = total

    def gather_copy(self, number, level, turn):
        _, device = self.peer(self.streams[number][level], turn)
        begin = self.starts[number][level + 1]
        extent = self.extents[number][level + 1]
        slot, _ = self.slots[number, level, turn]
        block = self.full.at[pl.ds(begin, extent)]
        return pltpu.make_async_remote_copy(
            src_ref=block,
            dst_ref=block,
            send_sem=self.sg.at[slot],
            recv_sem=self.rg.at[slot],
            device_id=device,
            device_id_type=pl.DeviceIdType.MESH,
        )

    def turns(self, number, level):
        return range(1, self.streams[number][level][2])

    def gather_start(self, number, level):
        for turn in self.turns(number, level):
            self.gather_copy(number, level, turn).start()

    def gather_finish(self, number, level):
        for turn in self.turns(number, level):
            self.gather_copy(number, level, turn).wait_recv()

    def clear(self):
        self.acc[...] = jnp.zeros_like(self.acc)

    def steps(self):
        numbers = range(len(self.streams))
        depth = len(self.streams[0])
        for number in numbers:
            self.scatter_start(number, 0)
        yield True
        for level in range(depth):
            for number in numbers:
                self.scatter_finish(number, level)
                if level + 1 < depth:
                    self.scatter_start(number, level + 1)
                else:
                    begin, extent = self.starts[number][-1], self.extents[number][-1]
                    mine = self.acc[pl.ds(2 * begin, 2 * extent)].astype(jnp.bfloat16)
                    self.full[pl.ds(begin, extent)] = mine.reshape(extent, TILE, LANES)
                    self.gather_start(number, level)
            yield True
        for level in reversed(range(depth)):
            for number in numbers:
                self.gather_finish(number, level)
                if level > 0:
                    self.gather_start(number, level - 1)
            yield True
        for number in numbers:
            for level in range(depth):
                for turn in self.turns(number, level):
                    self.scatter_copy(number, level, turn)[0].wait_send()
                    self.gather_copy(number, level, turn).wait_send()


def pack(acc, lane_tile, row_tile, block):
    rows, width = block.shape
    begin = lane_tile + row_tile
    acc[begin : begin + rows // 8, :, :width] = block.reshape(rows // 8, 8, width)


def lane_spans(width):
    return [(low, min(low + LANES, width)) for low in range(0, width, LANES)]


def window(main, edge, lane, shift):
    width = main.shape[1]
    if shift == 0:
        return main
    outside = lane < shift if shift > 0 else lane >= width + shift
    return pltpu.roll(jnp.where(outside, edge, main), (-shift) % width, 1)


class Halo:
    def __init__(self, sizes, margin, rows, channels, width):
        self.sizes, self.margin, self.rows = sizes, margin, rows
        self.channels, self.width = channels, width
        self.pitch = width // rows

    def scratch(self):
        packed = (self.channels, self.width)
        return [
            pltpu.VMEM(packed, jnp.bfloat16),
            pltpu.VMEM((2,) + packed, jnp.bfloat16),
            pltpu.VMEM(packed, jnp.bfloat16),
            pltpu.VMEM((2,) + packed, jnp.bfloat16),
            pltpu.VMEM((2, self.margin) + packed, jnp.bfloat16),
            pltpu.SemaphoreType.DMA((2,)),
            pltpu.SemaphoreType.DMA((2,)),
            pltpu.SemaphoreType.DMA((2,)),
            pltpu.SemaphoreType.DMA((2,)),
            pltpu.SemaphoreType.DMA((2,)),
            pltpu.SemaphoreType.DMA((2,)),
        ]

    def bind(self, cells, main, edge, pack_out, pack_in, corner_out, corner_in, strip_in, *sems):
        self.cells, self.main, self.edge = cells, main, edge
        self.pack_out, self.pack_in = pack_out, pack_in
        self.corner_out, self.corner_in, self.strip_in = corner_out, corner_in, strip_in
        lon, lat = lax.axis_index("lon"), lax.axis_index("lat")
        lons, lats = self.sizes["lon"], self.sizes["lat"]
        self.south_open = lat > 0
        self.top = lat == lats - 1
        mirror = lons - 1 - lon
        self.left = {"lon": lax.rem(lon + lons - 1, lons)}
        self.right = {"lon": lax.rem(lon + 1, lons)}
        self.peers = [self.left, self.right, {"lon": mirror}]
        up = {
            "lon": jnp.where(self.top, mirror, lon),
            "lat": jnp.where(self.top, lat, lat + 1),
        }
        down = {"lat": jnp.where(self.south_open, lat - 1, lat + 1)}
        slot = jnp.where(self.top, 1, 0)
        lon_send, lon_recv, strip_send, strip_recv, corner_send, corner_recv = sems
        self.lon_copies = [
            self.copy(pack_out, pack_in.at[0], lon_send.at[0], lon_recv.at[0], self.left)
        ]
        if lons > 2:
            self.lon_copies.append(
                self.copy(pack_out, pack_in.at[1], lon_send.at[1], lon_recv.at[1], self.right)
            )
        high = cells.at[pl.ds(self.rows - self.margin, self.margin)]
        low = cells.at[pl.ds(0, self.margin)]
        self.up_strip = self.copy(high, strip_in.at[slot], strip_send.at[0], strip_recv.at[slot], up)
        self.down_strip = self.copy(low, strip_in.at[1], strip_send.at[1], strip_recv.at[1], down)
        self.up_corner = self.copy(
            corner_out, corner_in.at[slot], corner_send.at[0], corner_recv.at[slot], up
        )
        self.down_corner = self.copy(
            corner_out, corner_in.at[1], corner_send.at[1], corner_recv.at[1], down
        )
        self.arrivals = [
            [
                self.copy(low, strip_in.at[side], strip_send.at[0], strip_recv.at[side], up),
                self.copy(corner_out, corner_in.at[side], corner_send.at[0], corner_recv.at[side], up),
            ]
            for side in range(2)
        ]
        self.lane = lax.broadcasted_iota(jnp.int32, (self.channels, self.width), 1)

    def copy(self, src, dst, send_sem, recv_sem, device):
        return pltpu.make_async_remote_copy(
            src_ref=src,
            dst_ref=dst,
            send_sem=send_sem,
            recv_sem=recv_sem,
            device_id=device,
            device_id_type=pl.DeviceIdType.MESH,
        )

    def pack_columns(self):
        packed = jnp.zeros((self.channels, self.width), jnp.float32)
        for row in range(self.rows):
            turned = pltpu.roll(
                self.cells[row].astype(jnp.float32), row * self.pitch + self.margin, 1
            )
            packed = jnp.where(self.lane >= row * self.pitch, turned, packed)
        self.pack_out[...] = packed.astype(jnp.bfloat16)

    def unpacked(self, packed, row):
        shift = (self.width - row * self.pitch - self.margin) % self.width
        return pltpu.roll(packed, shift, 1)

    def start(self):
        for copy in self.lon_copies:
            copy.start()
        self.up_strip.start()
        pl.when(self.south_open)(self.down_strip.start)

    def spread_rows(self):
        for row in range(self.rows):
            self.main[self.margin + row] = self.cells[row].astype(jnp.float32)

    def forward_corners(self):
        for copy in self.lon_copies:
            copy.wait_recv()
        packed = self.pack_in[0].astype(jnp.float32)
        if len(self.lon_copies) > 1:
            from_left = self.pack_in[1].astype(jnp.float32)
            packed = jnp.where(lax.rem(self.lane, self.pitch) < self.margin, from_left, packed)
        self.corner_out[...] = packed.astype(jnp.bfloat16)
        self.up_corner.start()
        pl.when(self.south_open)(self.down_corner.start)
        for row in range(self.rows):
            self.edge[self.margin + row] = self.unpacked(packed, row)

    def finish(self):
        margin, rows = self.margin, self.rows

        @pl.when(self.south_open)
        def _():
            for copy in self.arrivals[0]:
                copy.wait_recv()
            packed = self.corner_in[0].astype(jnp.float32)
            for at in range(margin):
                self.main[at] = self.strip_in[0, at].astype(jnp.float32)
                self.edge[at] = self.unpacked(packed, rows - margin + at)

        @pl.when(jnp.logical_not(self.south_open))
        def _():
            for at in range(margin):
                self.main[at] = jnp.zeros((self.channels, self.width), jnp.float32)
                self.edge[at] = jnp.zeros((self.channels, self.width), jnp.float32)

        for copy in self.arrivals[1]:
            copy.wait_recv()
        north = margin + rows

        @pl.when(self.top)
        def _():
            one = lax.broadcasted_iota(jnp.int32, (self.width, self.width), 0)
            two = lax.broadcasted_iota(jnp.int32, (self.width, self.width), 1)
            turn = jnp.where(one + two == self.width - 1, 1.0, 0.0).astype(jnp.bfloat16)
            packed = self.corner_in[1].astype(jnp.float32)
            for at in range(margin):
                self.main[north + at] = jnp.dot(
                    self.strip_in[1, margin - 1 - at], turn, preferred_element_type=jnp.float32
                )
                sides = self.unpacked(packed, rows - 1 - at).astype(jnp.bfloat16)
                self.edge[north + at] = jnp.dot(sides, turn, preferred_element_type=jnp.float32)

        @pl.when(jnp.logical_not(self.top))
        def _():
            packed = self.corner_in[1].astype(jnp.float32)
            for at in range(margin):
                self.main[north + at] = self.strip_in[1, at].astype(jnp.float32)
                self.edge[north + at] = self.unpacked(packed, at)

    def drain(self):
        for copy in self.lon_copies + [self.up_strip, self.up_corner]:
            copy.wait_send()
        pl.when(self.south_open)(self.down_strip.wait_send)
        pl.when(self.south_open)(self.down_corner.wait_send)


def block_kernel(
    big,
    small,
    halo,
    scale,
    cells_ref,
    cot_ref,
    mask_ref,
    dw_ref,
    gain_ref,
    expand_ref,
    reduce_t,
    state_out,
    expand_out,
    reduce_out,
    taps_out,
    gain_out,
    main_ref,
    edge_ref,
    expand_t,
    reduce_ref,
    table,
    table_t,
    conv,
    scaled_all,
    hidden_all,
    d_pre_all,
    gain_sum,
    *scratch,
):
    channels, hidden_units = expand_ref.shape
    eights = channels // 8
    margin = KS // 2
    tile_rows = main_ref.shape[0] - 2 * margin
    width = main_ref.shape[2]
    spans = lane_spans(hidden_units)
    big.bind(*scratch[:8])
    small.bind(*scratch[8:16])
    halo.bind(cells_ref, main_ref, edge_ref, *scratch[16:])
    peers = big.peers() + small.peers() + halo.peers
    barrier_count = len(peers)
    barrier = pltpu.get_barrier_semaphore()
    for device in peers:
        pl.semaphore_signal(
            barrier, inc=1, device_id=device, device_id_type=pl.DeviceIdType.MESH
        )
    halo.pack_columns()
    pl.semaphore_wait(barrier, barrier_count)
    halo.start()
    big.clear()
    small.clear()
    gain_sum[...] = jnp.zeros_like(gain_sum)
    for low, high in spans:
        piece = expand_ref[:, low:high].astype(jnp.float32).T
        expand_t[low:high, :] = piece.astype(jnp.bfloat16)
        piece = reduce_t[:, low:high].astype(jnp.float32).T
        reduce_ref[low:high, :] = piece.astype(jnp.bfloat16)
    table[...] = jnp.zeros_like(table)
    table[: KS * KS, :channels] = dw_ref[...]
    table[KS * KS : KS * KS + 1, :channels] = gain_ref[...]
    columns = table[...].T
    table_t[...] = columns
    gain = columns[:channels, KS * KS : KS * KS + 1]
    halo.spread_rows()
    halo.forward_corners()
    lane = lax.broadcasted_iota(jnp.int32, (8, width), 1)

    def conv_step(part, first, step, carry):
        rows = pl.ds(pl.multiple_of(step * 8, 8), 8)
        taps = table_t[rows, :]
        spans_of = [slice(row * width, (row + 1) * width) for row in range(tile_rows)]
        if first:
            sums = [jnp.zeros((8, width), jnp.float32) for _ in range(tile_rows)]
        else:
            sums = [conv[rows, one] for one in spans_of]
        for shift_b in range(KS):
            weights = [
                jnp.broadcast_to(taps[:, a * KS + shift_b : a * KS + shift_b + 1], (8, width))
                for a in range(KS)
            ]
            for row in part:
                cells = window(main_ref[row, rows, :], edge_ref[row, rows, :], lane, shift_b - margin)
                for shift_a in range(KS):
                    if 0 <= row - shift_a < tile_rows:
                        sums[row - shift_a] = sums[row - shift_a] + weights[shift_a] * cells
        for row in range(tile_rows):
            conv[rows, spans_of[row]] = sums[row]
        return carry

    halo.finish()
    every = range(tile_rows + 2 * margin)
    lax.fori_loop(0, eights, functools.partial(conv_step, every, True), 0)

    block_rows = 2
    block = block_rows * width

    def cell_step(step, carry):
        cells = pl.ds(pl.multiple_of(step * block, block), block)
        conv_blk = conv[:, cells]
        centred = conv_blk - jnp.mean(conv_blk, axis=0, keepdims=True)
        inv_std = lax.rsqrt(jnp.mean(centred * centred, axis=0, keepdims=True) + norm_eps)
        normed = centred * inv_std
        scaled = (normed * gain).astype(jnp.bfloat16)
        scaled_all[:, cells] = scaled
        pre_act = jnp.dot(expand_t[...], scaled, preferred_element_type=jnp.float32)
        normal_cdf = 0.5 * (1.0 + lax.erf(pre_act * root_half))
        normal_pdf = jnp.exp(-0.5 * pre_act * pre_act) * gauss_norm
        hidden = (pre_act * normal_cdf).astype(jnp.bfloat16)
        gelu_slope = normal_cdf + pre_act * normal_pdf
        d_hidden = jnp.dot(reduce_ref[...], cot_ref[:, cells], preferred_element_type=jnp.float32)
        d_pre = (d_hidden * gelu_slope).astype(jnp.bfloat16)
        hidden_all[:, cells] = hidden
        d_pre_all[:, cells] = d_pre
        branch = jnp.dot(reduce_t[...], hidden, preferred_element_type=jnp.float32)
        for part in range(block_rows):
            row = step * block_rows + part
            at = pl.ds(pl.multiple_of(row * width, width), width)
            total = main_ref[margin + row] + branch[:, part * width : (part + 1) * width]
            state_out[:, at] = (total * mask_ref[:, at]).astype(jnp.bfloat16)
        d_scaled = jnp.dot(expand_ref[...], d_pre, preferred_element_type=jnp.float32)
        product = d_scaled * normed
        for part in range(block_rows):
            gain_sum[...] += product[:, part * width : (part + 1) * width]
        d_normed = d_scaled * gain
        mean_one = jnp.mean(d_normed, axis=0, keepdims=True)
        mean_two = jnp.mean(d_normed * normed, axis=0, keepdims=True)
        conv[:, cells] = inv_std * (d_normed - mean_one - normed * mean_two)
        return carry

    lax.fori_loop(0, tile_rows // block_rows, cell_step, 0)

    over_cells = (((1,), (1,)), ((), ()))
    for low in range(0, hidden_units, 2 * LANES):
        high = min(low + 2 * LANES, hidden_units)
        for turn, (left, right) in enumerate([(scaled_all, d_pre_all), (cot_ref, hidden_all)]):
            grad = lax.dot_general(
                left[...], right[low:high, :], over_cells, preferred_element_type=jnp.float32
            )
            for first, last in lane_spans(high - low):
                at = (low + first) // LANES
                pack(big.acc, at * 2 * eights, turn * eights, grad[:, first:last] * scale)

    def depthwise_step(step, carry):
        rows = pl.ds(pl.multiple_of(step * 8, 8), 8)
        d_conv = [conv[rows, row * width : (row + 1) * width] for row in range(tile_rows)]
        line = jnp.sum(gain_sum[rows, :], axis=1, keepdims=True)
        line = jnp.where(lane == KS * KS, line, 0.0)
        for shift_b in range(KS):
            sums = [jnp.zeros((8, width), jnp.float32) for _ in range(KS)]
            for row in range(tile_rows + 2 * margin):
                cells = window(main_ref[row, rows, :], edge_ref[row, rows, :], lane, shift_b - margin)
                for shift_a in range(KS):
                    if 0 <= row - shift_a < tile_rows:
                        sums[shift_a] = sums[shift_a] + d_conv[row - shift_a] * cells
            for shift_a in range(KS):
                total = jnp.sum(sums[shift_a], axis=1, keepdims=True)
                line = jnp.where(lane == shift_a * KS + shift_b, total, line)
        small.acc[pl.ds(step, 1)] = (line[:, :LANES] * scale).reshape(1, 8, LANES)
        return carry

    ahead, behind = big.steps(), small.steps()
    next(ahead)
    lax.fori_loop(0, eights // 2, depthwise_step, 0)
    next(ahead)
    lax.fori_loop(eights // 2, eights, depthwise_step, 0)
    running = [behind, ahead]
    while running:
        running = [one for one in running if next(one, None) is not None]

    for at, (low, high) in enumerate(spans):
        both = big.full[at * eights : (at + 1) * eights].astype(jnp.float32)
        both = both.reshape(2 * channels, LANES)
        expand_out[:, low:high] = both[:channels, : high - low]
        reduce_out[:, low:high] = both[channels:, : high - low]
    table_t[:channels] = (
        small.full[: -(-eights // 2)].astype(jnp.float32).reshape(-1, LANES)[:channels]
    )
    lines = table_t[...].T
    taps_out[...] = lines[: KS * KS, :channels]
    gain_out[...] = lines[KS * KS : KS * KS + 1, :channels]
    halo.drain()


def block_call(sizes, scale, masked, cot, mask, dw_weight, norm_gain, expand_weight, reduce_weight):
    channels, hidden = expand_weight.shape
    cells = cot.shape[1]
    eights = channels // 8
    big = Reducer(sizes, big_streams(sizes), -(-hidden // LANES) * eights)
    small = Reducer(sizes, small_streams(sizes), -(-eights // 2))
    rows, _, width = masked.shape
    halo = Halo(sizes, KS // 2, rows, channels, width)
    padded = pltpu.VMEM((rows + 2 * (KS // 2), channels, width), jnp.float32)
    vmem = pl.BlockSpec(memory_space=pltpu.VMEM)
    return pl.pallas_call(
        functools.partial(block_kernel, big, small, halo, scale),
        out_shape=(
            jax.ShapeDtypeStruct((channels, cells), jnp.bfloat16),
            jax.ShapeDtypeStruct((channels, hidden), jnp.float32),
            jax.ShapeDtypeStruct((channels, hidden), jnp.float32),
            jax.ShapeDtypeStruct((KS * KS, channels), jnp.float32),
            jax.ShapeDtypeStruct((1, channels), jnp.float32),
        ),
        in_specs=[vmem] * 7,
        out_specs=[vmem] * 5,
        scratch_shapes=[
            padded,
            padded,
            pltpu.VMEM((hidden, channels), jnp.bfloat16),
            pltpu.VMEM((hidden, channels), jnp.bfloat16),
            pltpu.VMEM((LANES, -(-channels // LANES) * LANES), jnp.float32),
            pltpu.VMEM((-(-channels // LANES) * LANES, LANES), jnp.float32),
            pltpu.VMEM((channels, cells), jnp.float32),
            pltpu.VMEM((channels, cells), jnp.bfloat16),
            pltpu.VMEM((hidden, cells), jnp.bfloat16),
            pltpu.VMEM((hidden, cells), jnp.bfloat16),
            pltpu.VMEM((channels, width), jnp.float32),
        ]
        + big.scratch()
        + small.scratch()
        + halo.scratch(),
        compiler_params=pltpu.CompilerParams(
            collective_id=0, has_side_effects=True, vmem_limit_bytes=60 * 1024 * 1024
        ),
    )(masked, cot, mask, dw_weight.T, norm_gain[None, :], expand_weight, reduce_weight.T)


def body(ocean_state, ocean_mask, dw_weight, norm_gain, expand_weight, reduce_weight, cotangent):
    state_tile = ocean_state[0]
    channels, tile_rows, tile_cols = state_tile.shape
    mask_bf = ocean_mask.astype(jnp.bfloat16)
    masked = (state_tile * mask_bf[None]).transpose(1, 0, 2)
    cell_count = tile_rows * tile_cols
    cot_masked = (cotangent[0] * mask_bf[None]).reshape(channels, cell_count)
    sizes = {axis: lax.axis_size(axis) for axis in MESH_AXES}
    grad_scale = 1.0 / math.sqrt(math.prod(sizes.values()) * cell_count)
    out_flat, grad_expand, grad_reduce, taps, gain = block_call(
        sizes,
        grad_scale,
        masked,
        cot_masked,
        ocean_mask.astype(jnp.float32).reshape(1, cell_count),
        dw_weight,
        norm_gain,
        expand_weight,
        reduce_weight,
    )
    next_state = out_flat.reshape(channels, tile_rows, tile_cols)[None]
    return (next_state, taps.T, gain[0], grad_expand, grad_reduce.T)


def solution(mesh):
    return jax.shard_map(
        body,
        mesh=mesh,
        in_specs=(
            P("ens", None, "lat", "lon"),
            P("lat", "lon"),
            P(),
            P(),
            P(),
            P(),
            P("ens", None, "lat", "lon"),
        ),
        out_specs=(P("ens", None, "lat", "lon"), P(), P(), P(), P()),
        check_vma=False,
    )
```
